32 devices in a mesh: section: 2 (over core), ctx: 4 (over z), mp: 4 (over y, x).
Axes of the slice: x: 2, y: 2, z: 4, core: 2. Of those that a mesh axis runs over, the one named last changes fastest.
Arguments:
- hidden: bfloat16 [2, 512, 4672], P('section', 'ctx', 'mp'), may hold values from -120 to 120
- query: bfloat16 [2, 512, 2048], P('section', 'ctx', 'mp'), may hold values from -6 to 6
- keys: bfloat16 [2, 512, 2048], P('section', 'ctx', 'mp'), may hold values from -100 to 100
- values: bfloat16 [2, 512, 2048], P('section', 'ctx', 'mp'), may hold values from -12 to 12
- w_out: bfloat16 [2, 4672, 2048], P('section', 'ctx', 'mp'), may hold values from -0.125 to 0.125
Outputs:
- handed: bfloat16 [2, 512, 4672], P('section', 'ctx', 'mp')
- context: bfloat16 [2, 512, 2048], P('section', 'ctx', 'mp')
The draws below stay inside these ranges and needn't reach their ends.
All inputs are finite; a program needn't handle non-finite values.
Results may differ from the reference program's by a relative error of at most 0.0075.
Values may be sent and summed in bfloat16 or wider, within the bound.
A program may use at most 128 MiB of HBM per device.

```python
import math
import jax
import jax.numpy as jnp
from jax import lax

D = 4672
HEADS = 32
HEAD_DIM = 64
SECTIONS = 2
DEC = 512
ENC = 512
INNER = 2048
INNER_DEV = 512
N_MP = 4


def draw_hidden(key, part):
    key_base, key_rows = jax.random.split(jax.random.fold_in(key, 11))
    columns = jnp.exp(math.log(3.0) * jnp.arange(D, dtype=jnp.float32) / (D - 1))
    base = jnp.clip(jax.random.normal(key_base, (SECTIONS, DEC, D), jnp.float32), -4.0, 4.0)
    row_scale = jnp.exp(jax.random.uniform(key_rows, (SECTIONS, DEC, 1), jnp.float32, 0.0, math.log(10.0)))
    return (base * row_scale * columns).astype(jnp.bfloat16)


def draw_keys(key, part):
    key_base = jax.random.fold_in(jax.random.fold_in(key, 23), 0)
    base = 0.3 * jnp.clip(jax.random.normal(key_base, (SECTIONS, ENC, INNER), jnp.float32), -4.0, 4.0)
    return base.astype(jnp.bfloat16)


def steps_of(key, dims, cuts, smallest, high):
    loudness = 1.0
    for dim, shards_of in cuts:
        draws = jax.random.uniform(jax.random.fold_in(jax.random.fold_in(key, 6), dim), (shards_of,), jnp.float32, smallest / len(cuts), high / len(cuts))
        loudness = loudness * jnp.repeat(jnp.exp(draws), dims[dim] // shards_of).reshape((-1,) + (1,) * (len(dims) - 1 - dim))
    return loudness


def bell_draw(own_key, shape, deviation, most, cuts=(), held_as=jnp.bfloat16):
    values = deviation * jax.random.normal(own_key, shape, jnp.float32)
    if cuts:
        values = values * steps_of(own_key, shape, cuts, -0.22, 0.18)
    return jnp.clip(values, -most, most).astype(held_as)


def setup_inputs(seed: int = 0) -> dict:
    splits = jax.random.split(jax.random.key(seed), 6)
    return {
        "hidden": draw_hidden(jax.random.fold_in(splits[5], 71), 0),
        "query": bell_draw(splits[1], (SECTIONS, DEC, INNER), 1.0, 6.0, ((0, 2), (1, 4), (2, 4))),
        "keys": draw_keys(jax.random.fold_in(splits[5], 71), 0),
        "values": bell_draw(splits[3], (SECTIONS, ENC, INNER), 3.0, 12.0, ((0, 2), (1, 4), (2, 4))),
        "w_out": bell_draw(splits[4], (SECTIONS, D, INNER), INNER ** -0.5, 0.125, ((0, 2), (1, 4), (2, 4))),
    }


def attend_head(parts):
    query_h, keys_h, values_h = parts
    scores = jnp.dot(query_h, keys_h.T, preferred_element_type=jnp.float32)
    peak = jnp.max(scores, axis=1, keepdims=True)
    expo = jnp.exp(scores - peak)
    total = jnp.sum(expo, axis=1, keepdims=True)
    return jnp.dot(expo.astype(jnp.bfloat16), values_h, preferred_element_type=jnp.float32) / total


def split_heads(matrix):
    return jnp.transpose(matrix.reshape(matrix.shape[0], HEADS, HEAD_DIM), (1, 0, 2))


def one_layer(parts):
    hidden_l, query_l, keys_l, values_l, out_w = parts
    rows_f = hidden_l.astype(jnp.float32)
    per_head = lax.map(attend_head, (split_heads(query_l), split_heads(keys_l), split_heads(values_l)))
    context = jnp.transpose(per_head, (1, 0, 2)).reshape(query_l.shape[0], HEADS * HEAD_DIM).astype(jnp.bfloat16)
    grouped = context.reshape(context.shape[0], N_MP, INNER_DEV).astype(jnp.float32)
    out_grouped = out_w.reshape(out_w.shape[0], N_MP, INNER_DEV).astype(jnp.float32)
    partial_terms = jnp.einsum("rgw,dgw->grd", grouped, out_grouped).astype(jnp.bfloat16)
    partial_terms = lax.optimization_barrier(partial_terms)
    branch = jnp.sum(partial_terms.astype(jnp.float32), axis=0)
    result = (rows_f + branch).astype(jnp.bfloat16)
    return result, context


def reference(hidden, query, keys, values, w_out):
    outputs, context = lax.map(one_layer, (hidden, query, keys, values, w_out))
    handed = jnp.roll(outputs, 1, axis=0)
    return handed, context
```

```python
import functools

import jax
import jax.numpy as jnp
from jax import lax
from jax.experimental import pallas as pl
from jax.experimental.pallas import tpu as pltpu
from jax.sharding import PartitionSpec as P

HEAD_DIM = 64
MESH = pl.DeviceIdType.MESH
NT = (((1,), (1,)), ((), ()))


def dot(a, b, dims=(((1,), (0,)), ((), ()))):
    return lax.dot_general(a, b, dims, preferred_element_type=jnp.float32)


def relay_kernel(
    n,
    order,
    q_hbm,
    k_hbm,
    v_hbm,
    w_hbm,
    hid_hbm,
    branch_out,
    hid_out,
    ctx_out,
    qkv,
    w,
    expo,
    total,
    ctx,
    part,
    red,
    zsrc,
    zin,
    local_sem,
    qkv_send,
    qkv_recv,
    hid_sem,
    ctx_send,
    ctx_recv,
    red_send,
    red_recv,
    z_send,
    z_recv,
    out_send,
    out_recv,
):
    s = lax.axis_index("section")
    c = lax.axis_index("ctx")
    m = lax.axis_index("mp")
    other = 1 - s
    wide = ctx.shape[2] // n
    rows = ctx.shape[1]
    cut = rows // n

    def columns(j):
        return pl.ds(pl.multiple_of(j * wide, wide), wide)

    def send(src, dst, send_sem, recv_sem, device):
        copy = pltpu.make_async_remote_copy(
            src_ref=src,
            dst_ref=dst,
            send_sem=send_sem,
            recv_sem=recv_sem,
            device_id=device,
            device_id_type=MESH,
        )
        copy.start()
        return copy

    inputs = (k_hbm, q_hbm, v_hbm)
    own = []
    for i, ref in enumerate(inputs):
        own.append(pltpu.make_async_copy(ref.at[:, columns(c)], qkv.at[i, c], local_sem.at[i]))
    own.append(pltpu.make_async_copy(w_hbm, w, local_sem.at[3]))
    for copy in own:
        copy.start()

    barrier = pltpu.get_barrier_semaphore()
    for d in range(1, n):
        pl.semaphore_signal(barrier, inc=1, device_id=(s, lax.rem(c + d, n), m), device_id_type=MESH)
        pl.semaphore_signal(barrier, inc=1, device_id=(s, c, lax.rem(m + d, n)), device_id_type=MESH)
    for a in range(n):
        pl.semaphore_signal(barrier, inc=1, device_id=(other, c, a), device_id_type=MESH)
    pl.semaphore_wait(barrier, 3 * n - 2)

    qkv_copies = []
    for i, ref in enumerate(inputs):
        group = []
        for d in range(1, n):
            j = lax.rem(c + d, n)
            group.append(
                send(ref.at[:, columns(j)], qkv.at[i, c], qkv_send.at[i, d - 1], qkv_recv.at[i, d - 1], (s, j, m))
            )
        qkv_copies.append(group)
    hid_copy = send(hid_hbm, hid_out, hid_sem.at[0], hid_sem.at[1], (other, c, m))

    lane = lax.broadcasted_iota(jnp.int32, (rows, wide), 1) // HEAD_DIM
    heads = wide // HEAD_DIM
    masks = [jnp.where(lane == h, 1.0, 0.0).astype(jnp.bfloat16) for h in range(heads)]
    for i in (0, 1):
        own[i].wait()
        for copy in qkv_copies[i]:
            copy.wait_recv()
    keys_all = qkv[0].reshape(n * rows, wide)
    for r in order:
        q_r = qkv[1, r]
        scores = dot(jnp.concatenate([q_r * mask for mask in masks], axis=0), keys_all, NT)
        e = jnp.exp(scores - jnp.max(scores, axis=1, keepdims=True))
        sums = jnp.sum(e, axis=1, keepdims=True)
        wide_sum = jnp.broadcast_to(sums[:rows], (rows, wide))
        for h in range(1, heads):
            wide_sum = jnp.where(lane == h, sums[h * rows : (h + 1) * rows], wide_sum)
        total[r] = wide_sum
        expo[r] = e.astype(jnp.bfloat16)

    own[2].wait()
    for copy in qkv_copies[2]:
        copy.wait_recv()
    values_all = qkv[2].reshape(n * rows, wide)
    ctx_copies = {}
    for r in order:
        both = dot(expo[r], values_all)
        picked = both[:rows]
        for h in range(1, heads):
            picked = jnp.where(lane == h, both[h * rows : (h + 1) * rows], picked)
        ctx[r, :, columns(c)] = (picked / total[r]).astype(jnp.bfloat16)
        ctx_copies[r] = [
            send(
                ctx.at[r, :, columns(c)],
                ctx.at[r, :, columns(c)],
                ctx_send.at[r, d - 1],
                ctx_recv.at[r, d - 1],
                (s, lax.rem(c + d, n), m),
            )
            for d in range(1, n)
        ]

    own[3].wait()
    red_copies = {}

    def project(r):
        for copy in ctx_copies[r]:
            copy.wait_recv()
        part[r] = dot(ctx[r], w[...], NT).astype(jnp.bfloat16).reshape(part.shape[1:])
        group = []
        for d in range(1, n):
            t = lax.rem(m + d, n)
            group.append(
                send(part.at[r, t], red.at[r, d - 1], red_send.at[r, d - 1], red_recv.at[r, d - 1], (s, c, t))
            )
        red_copies[r] = group

    def z_copy(r):
        return pltpu.make_async_remote_copy(
            src_ref=zsrc.at[r],
            dst_ref=zin.at[c],
            send_sem=z_send.at[r],
            recv_sem=z_recv.at[c],
            device_id=(s, r, m),
            device_id_type=MESH,
        )

    def reduce(r):
        for copy in red_copies[r]:
            copy.wait_recv()
        acc = part[r, m].astype(jnp.float32)
        for d in range(1, n):
            acc = acc + red[r, d - 1].astype(jnp.float32)
        acc = acc.astype(jnp.bfloat16)

        @pl.when(c == r)
        def _():
            zin[c] = acc

        @pl.when(c != r)
        def _():
            zsrc[r] = acc
            z_copy(r).start()

    project(order[0])
    for i in range(1, n):
        project(order[i])
        reduce(order[i - 1])
    ctx_back = pltpu.make_async_copy(ctx.at[c], ctx_out, local_sem.at[4])
    ctx_back.start()
    reduce(order[n - 1])

    out_copies = []
    for step in range(n):
        a = lax.rem(c + step, n)
        if step:
            pltpu.make_async_remote_copy(
                src_ref=zsrc.at[0],
                dst_ref=zin.at[a],
                send_sem=z_send.at[0],
                recv_sem=z_recv.at[a],
                device_id=(s, a, m),
                device_id_type=MESH,
            ).wait_recv()
        out_copies.append(
            send(
                zin.at[a],
                branch_out.at[pl.ds(pl.multiple_of(m * cut, cut), cut)],
                out_send.at[step],
                out_recv.at[m],
                (other, c, a),
            )
        )

    ctx_back.wait()
    for group in qkv_copies + list(ctx_copies.values()) + list(red_copies.values()):
        for copy in group:
            copy.wait_send()
    hid_copy.wait()
    for r in range(n):
        pl.when(c != r)(z_copy(r).wait_send)
    for copy in out_copies:
        copy.wait_send()
    for g in range(n):
        pltpu.make_async_remote_copy(
            src_ref=zin.at[0],
            dst_ref=branch_out.at[pl.ds(g * cut, cut)],
            send_sem=out_send.at[0],
            recv_sem=out_recv.at[g],
            device_id=(other, c, g),
            device_id_type=MESH,
        ).wait_recv()


def relay_body(n, hidden, query, keys, values, w_out):
    rows, inner = query.shape[1:]
    depth = hidden.shape[2]
    wide = inner // n
    heads = wide // HEAD_DIM
    cut = rows // n
    order = sorted(range(n), key=lambda r: (-abs(2 * r - n + 1), r))
    bf16 = jnp.bfloat16
    dma = pltpu.SemaphoreType.DMA
    any_spec = pl.BlockSpec(memory_space=pl.ANY)
    branch, carried, context = pl.pallas_call(
        functools.partial(relay_kernel, n, order),
        out_shape=(
            jax.ShapeDtypeStruct((rows, depth), bf16),
            jax.ShapeDtypeStruct((rows, depth), bf16),
            jax.ShapeDtypeStruct((rows, inner), bf16),
        ),
        in_specs=[any_spec] * 5,
        out_specs=(any_spec,) * 3,
        scratch_shapes=[
            pltpu.VMEM((3, n, rows, wide), bf16),
            pltpu.VMEM((depth, inner), bf16),
            pltpu.VMEM((n, heads * rows, n * rows), bf16),
            pltpu.VMEM((n, rows, wide), jnp.float32),
            pltpu.VMEM((n, rows, inner), bf16),
            pltpu.VMEM((n, n, cut, depth), bf16),
            pltpu.VMEM((n, n - 1, cut, depth), bf16),
            pltpu.VMEM((n, cut, depth), bf16),
            pltpu.VMEM((n, cut, depth), bf16),
            dma((5,)),
            dma((3, n - 1)),
            dma((3, n - 1)),
            dma((2,)),
            dma((n, n - 1)),
            dma((n, n - 1)),
            dma((n, n - 1)),
            dma((n, n - 1)),
            dma((n,)),
            dma((n,)),
            dma((n,)),
            dma((n,)),
        ],
        compiler_params=pltpu.CompilerParams(
            collective_id=0, has_side_effects=True, vmem_limit_bytes=32 * 2**20
        ),
    )(query[0], keys[0], values[0], w_out[0], hidden[0])
    handed = (carried.astype(jnp.float32) + branch.astype(jnp.float32)).astype(bf16)
    return (handed[None], context[None])


def from_behind(block, axis, distance):
    devices = range(lax.axis_size(axis))
    route = [((i - distance) % len(devices), i) for i in devices]
    return lax.ppermute(block, axis, route)


def head_scores(query_h, keys_h):
    return jnp.einsum("qd,kd->qk", query_h, keys_h, preferred_element_type=jnp.float32)


def body(hidden, query, keys, values, w_out):
    n = lax.axis_size("ctx")
    square = lax.axis_size("mp") == n and lax.axis_size("section") == 2
    if square and query.shape[2] % (128 * n) == 0 and query.shape[1] % (16 * n) == 0:
        return relay_body(n, hidden, query, keys, values, w_out)
    rows = hidden[0]
    query_rows = query[0]
    inner_dev = query_rows.shape[1]
    heads_dev = inner_dev // HEAD_DIM
    keys_local = keys[0]
    values_local = values[0]
    keys_all, values_all = (
        lax.all_gather(keys_local, "ctx", axis=0, tiled=True),
        lax.all_gather(values_local, "ctx", axis=0, tiled=True),
    )
    pieces = []
    for head in range(heads_dev):
        lower = head * HEAD_DIM
        upper = lower + HEAD_DIM
        scores = head_scores(query_rows[:, lower:upper], keys_all[:, lower:upper])
        peak = jnp.max(scores, axis=1, keepdims=True)
        expo = jnp.exp(scores - peak)
        total = jnp.sum(expo, axis=1, keepdims=True)
        summed = jnp.dot(
            expo.astype(jnp.bfloat16),
            values_all[:, lower:upper],
            preferred_element_type=jnp.float32,
        )
        pieces.append(summed / total)
    context = jnp.concatenate(pieces, axis=1).astype(jnp.bfloat16)
    out_local = w_out[0]
    context_all = lax.all_gather(context, "ctx", axis=0, tiled=True)
    projected = jnp.einsum(
        "ri,di->rd", context_all, out_local, preferred_element_type=jnp.float32
    ).astype(jnp.bfloat16)
    branch_terms = lax.all_to_all(projected, "ctx", split_axis=0, concat_axis=1, tiled=True).astype(
        jnp.float32
    )
    branch = lax.psum_scatter(
        branch_terms.astype(jnp.bfloat16), "mp", scatter_dimension=1, tiled=True
    ).astype(jnp.float32)
    result = (rows.astype(jnp.float32) + branch).astype(jnp.bfloat16)
    handed = from_behind(result, "section", 1)
    return (handed[None], context[None])


def solution(mesh):
    in_specs = (
        P("section", "ctx", "mp"),
        P("section", "ctx", "mp"),
        P("section", "ctx", "mp"),
        P("section", "ctx", "mp"),
        P("section", "ctx", "mp"),
    )
    out_specs = (P("section", "ctx", "mp"), P("section", "ctx", "mp"))
    return jax.shard_map(body, mesh=mesh, in_specs=in_specs, out_specs=out_specs, check_vma=False)
```

```python
import functools

import jax
import jax.numpy as jnp
from jax import lax
from jax.experimental import pallas as pl
from jax.experimental.pallas import tpu as pltpu
from jax.sharding import PartitionSpec as P

HEAD_DIM = 64
MESH = pl.DeviceIdType.MESH
NT = (((1,), (1,)), ((), ()))


def dot(a, b, dims=(((1,), (0,)), ((), ()))):
    return lax.dot_general(a, b, dims, preferred_element_type=jnp.float32)


def relay_kernel(
    n,
    order,
    q_hbm,
    k_hbm,
    v_hbm,
    w_hbm,
    hid_hbm,
    branch_out,
    hid_out,
    ctx_out,
    qkv,
    w,
    expo,
    total,
    ctx,
    part,
    red,
    zsrc,
    zin,
    local_sem,
    qkv_send,
    qkv_recv,
    hid_sem,
    ctx_send,
    ctx_recv,
    red_send,
    red_recv,
    z_send,
    z_recv,
    out_send,
    out_recv,
):
    s = lax.axis_index("section")
    c = lax.axis_index("ctx")
    m = lax.axis_index("mp")
    other = 1 - s
    wide = ctx.shape[2] // n
    rows = ctx.shape[1]
    depth = w_hbm.shape[0]
    cut = zsrc.shape[1]

    def columns(j):
        return pl.ds(pl.multiple_of(j * wide, wide), wide)

    def send(src, dst, send_sem, recv_sem, device):
        copy = pltpu.make_async_remote_copy(
            src_ref=src,
            dst_ref=dst,
            send_sem=send_sem,
            recv_sem=recv_sem,
            device_id=device,
            device_id_type=MESH,
        )
        copy.start()
        return copy

    inputs = (k_hbm, q_hbm, v_hbm)
    own = []
    for i, ref in enumerate(inputs):
        own.append(pltpu.make_async_copy(ref.at[:, columns(c)], qkv.at[i, c], local_sem.at[i]))
    own.append(pltpu.make_async_copy(w_hbm, w.at[pl.ds(0, depth)], local_sem.at[3]))
    for copy in own:
        copy.start()

    if n * cut > depth:
        w[depth:] = jnp.zeros((n * cut - depth, w.shape[1]), w.dtype)

    barrier = pltpu.get_barrier_semaphore()
    for d in range(1, n):
        pl.semaphore_signal(barrier, inc=1, device_id=(s, lax.rem(c + d, n), m), device_id_type=MESH)
        pl.semaphore_signal(barrier, inc=1, device_id=(s, c, lax.rem(m + d, n)), device_id_type=MESH)
    for a in range(n):
        pl.semaphore_signal(barrier, inc=1, device_id=(other, c, a), device_id_type=MESH)
    pl.semaphore_wait(barrier, 3 * n - 2)

    qkv_copies = []
    for i, ref in enumerate(inputs):
        group = []
        for d in range(1, n):
            j = lax.rem(c + d, n)
            group.append(
                send(ref.at[:, columns(j)], qkv.at[i, c], qkv_send.at[i, d - 1], qkv_recv.at[i, d - 1], (s, j, m))
            )
        qkv_copies.append(group)
    hid_copy = send(hid_hbm, hid_out, hid_sem.at[0], hid_sem.at[1], (other, c, m))

    lane = lax.broadcasted_iota(jnp.int32, (rows, wide), 1) // HEAD_DIM
    heads = wide // HEAD_DIM
    masks = [jnp.where(lane == h, 1.0, 0.0).astype(jnp.bfloat16) for h in range(heads)]
    for i in (0, 1):
        own[i].wait()
        for copy in qkv_copies[i]:
            copy.wait_recv()
    keys_all = qkv[0].reshape(n * rows, wide)
    for r in order:
        q_r = qkv[1, r]
        scores = dot(jnp.concatenate([q_r * mask for mask in masks], axis=0), keys_all, NT)
        e = jnp.exp(scores - jnp.max(scores, axis=1, keepdims=True))
        sums = jnp.sum(e, axis=1, keepdims=True)
        wide_sum = jnp.broadcast_to(sums[:rows], (rows, wide))
        for h in range(1, heads):
            wide_sum = jnp.where(lane == h, sums[h * rows : (h + 1) * rows], wide_sum)
        total[r] = wide_sum
        expo[r] = e.astype(jnp.bfloat16)

    own[2].wait()
    for copy in qkv_copies[2]:
        copy.wait_recv()
    values_all = qkv[2].reshape(n * rows, wide)
    ctx_copies = {}
    for r in order:
        both = dot(expo[r], values_all)
        picked = both[:rows]
        for h in range(1, heads):
            picked = jnp.where(lane == h, both[h * rows : (h + 1) * rows], picked)
        ctx[r, :, columns(c)] = (picked / total[r]).astype(jnp.bfloat16)
        ctx_copies[r] = [
            send(
                ctx.at[r, :, columns(c)],
                ctx.at[r, :, columns(c)],
                ctx_send.at[r, d - 1],
                ctx_recv.at[r, d - 1],
                (s, lax.rem(c + d, n), m),
            )
            for d in range(1, n)
        ]

    own[3].wait()
    red_copies = {}

    def project(r):
        for copy in ctx_copies[r]:
            copy.wait_recv()
        part[r] = dot(w[...], ctx[r], NT).astype(jnp.bfloat16).reshape(part.shape[1:])
        group = []
        for d in range(1, n):
            t = lax.rem(m + d, n)
            group.append(
                send(part.at[r, t], red.at[r, d - 1], red_send.at[r, d - 1], red_recv.at[r, d - 1], (s, c, t))
            )
        red_copies[r] = group

    def z_copy(r):
        return pltpu.make_async_remote_copy(
            src_ref=zsrc.at[r],
            dst_ref=zin.at[c],
            send_sem=z_send.at[r],
            recv_sem=z_recv.at[c],
            device_id=(s, r, m),
            device_id_type=MESH,
        )

    def reduce(r):
        for copy in red_copies[r]:
            copy.wait_recv()
        acc = part[r, m].astype(jnp.float32)
        for d in range(1, n):
            acc = acc + red[r, d - 1].astype(jnp.float32)
        acc = acc.astype(jnp.bfloat16)

        @pl.when(c == r)
        def _():
            zin[c] = acc

        @pl.when(c != r)
        def _():
            zsrc[r] = acc
            z_copy(r).start()

    project(order[0])
    for i in range(1, n):
        project(order[i])
        reduce(order[i - 1])
    ctx_back = pltpu.make_async_copy(ctx.at[c], ctx_out, local_sem.at[4])
    ctx_back.start()
    reduce(order[n - 1])

    out_copies = []
    for step in range(n):
        a = lax.rem(c + step, n)
        if step:
            pltpu.make_async_remote_copy(
                src_ref=zsrc.at[0],
                dst_ref=zin.at[a],
                send_sem=z_send.at[0],
                recv_sem=z_recv.at[a],
                device_id=(s, a, m),
                device_id_type=MESH,
            ).wait_recv()
        out_copies.append(
            send(
                zin.at[a],
                branch_out.at[pl.ds(pl.multiple_of(m * cut, cut), cut)],
                out_send.at[step],
                out_recv.at[m],
                (other, c, a),
            )
        )

    ctx_back.wait()
    for group in qkv_copies + list(ctx_copies.values()) + list(red_copies.values()):
        for copy in group:
            copy.wait_send()
    hid_copy.wait()
    for r in range(n):
        pl.when(c != r)(z_copy(r).wait_send)
    for copy in out_copies:
        copy.wait_send()
    for g in range(n):
        pltpu.make_async_remote_copy(
            src_ref=zin.at[0],
            dst_ref=branch_out.at[pl.ds(g * cut, cut)],
            send_sem=out_send.at[0],
            recv_sem=out_recv.at[g],
            device_id=(other, c, g),
            device_id_type=MESH,
        ).wait_recv()


def relay_body(n, hidden, query, keys, values, w_out):
    rows, inner = query.shape[1:]
    depth = hidden.shape[2]
    wide = inner // n
    heads = wide // HEAD_DIM
    cut = -(-depth // (16 * n)) * 16
    order = sorted(range(n), key=lambda r: (-abs(2 * r - n + 1), r))
    bf16 = jnp.bfloat16
    dma = pltpu.SemaphoreType.DMA
    hbm = pl.BlockSpec(memory_space=pltpu.HBM)
    branch, carried, context = pl.pallas_call(
        functools.partial(relay_kernel, n, order),
        out_shape=(
            jax.ShapeDtypeStruct((n * cut, rows), bf16),
            jax.ShapeDtypeStruct((depth, rows), bf16),
            jax.ShapeDtypeStruct((rows, inner), bf16),
        ),
        in_specs=[hbm] * 5,
        out_specs=(hbm,) * 3,
        scratch_shapes=[
            pltpu.VMEM((3, n, rows, wide), bf16),
            pltpu.VMEM((n * cut, inner), bf16),
            pltpu.VMEM((n, heads * rows, n * rows), bf16),
            pltpu.VMEM((n, rows, wide), jnp.float32),
            pltpu.VMEM((n, rows, inner), bf16),
            pltpu.VMEM((n, n, cut, rows), bf16),
            pltpu.VMEM((n, n - 1, cut, rows), bf16),
            pltpu.VMEM((n, cut, rows), bf16),
            pltpu.VMEM((n, cut, rows), bf16),
            dma((5,)),
            dma((3, n - 1)),
            dma((3, n - 1)),
            dma((2,)),
            dma((n, n - 1)),
            dma((n, n - 1)),
            dma((n, n - 1)),
            dma((n, n - 1)),
            dma((n,)),
            dma((n,)),
            dma((n,)),
            dma((n,)),
        ],
        compiler_params=pltpu.CompilerParams(
            collective_id=0, has_side_effects=True, vmem_limit_bytes=60 * 2**20
        ),
    )(query[0], keys[0], values[0], w_out[0], hidden[0].T)
    handed = (carried.astype(jnp.float32) + branch[:depth].astype(jnp.float32)).astype(bf16)
    return (handed.T[None], context[None])


def from_behind(block, axis, distance):
    devices = range(lax.axis_size(axis))
    route = [((i - distance) % len(devices), i) for i in devices]
    return lax.ppermute(block, axis, route)


def head_scores(query_h, keys_h):
    return jnp.einsum("qd,kd->qk", query_h, keys_h, preferred_element_type=jnp.float32)


def body(hidden, query, keys, values, w_out):
    n = lax.axis_size("ctx")
    square = lax.axis_size("mp") == n and lax.axis_size("section") == 2
    if square and query.shape[2] % (128 * n) == 0 and query.shape[1] % 128 == 0:
        return relay_body(n, hidden, query, keys, values, w_out)
    rows = hidden[0]
    query_rows = query[0]
    inner_dev = query_rows.shape[1]
    heads_dev = inner_dev // HEAD_DIM
    keys_local = keys[0]
    values_local = values[0]
    keys_all, values_all = (
        lax.all_gather(keys_local, "ctx", axis=0, tiled=True),
        lax.all_gather(values_local, "ctx", axis=0, tiled=True),
    )
    pieces = []
    for head in range(heads_dev):
        lower = head * HEAD_DIM
        upper = lower + HEAD_DIM
        scores = head_scores(query_rows[:, lower:upper], keys_all[:, lower:upper])
        peak = jnp.max(scores, axis=1, keepdims=True)
        expo = jnp.exp(scores - peak)
        total = jnp.sum(expo, axis=1, keepdims=True)
        summed = jnp.dot(
            expo.astype(jnp.bfloat16),
            values_all[:, lower:upper],
            preferred_element_type=jnp.float32,
        )
        pieces.append(summed / total)
    context = jnp.concatenate(pieces, axis=1).astype(jnp.bfloat16)
    out_local = w_out[0]
    context_all = lax.all_gather(context, "ctx", axis=0, tiled=True)
    projected = jnp.einsum(
        "ri,di->rd", context_all, out_local, preferred_element_type=jnp.float32
    ).astype(jnp.bfloat16)
    branch_terms = lax.all_to_all(projected, "ctx", split_axis=0, concat_axis=1, tiled=True).astype(
        jnp.float32
    )
    branch = lax.psum_scatter(
        branch_terms.astype(jnp.bfloat16), "mp", scatter_dimension=1, tiled=True
    ).astype(jnp.float32)
    result = (rows.astype(jnp.float32) + branch).astype(jnp.bfloat16)
    handed = from_behind(result, "section", 1)
    return (handed[None], context[None])


def solution(mesh):
    in_specs = (
        P("section", "ctx", "mp"),
        P("section", "ctx", "mp"),
        P("section", "ctx", "mp"),
        P("section", "ctx", "mp"),
        P("section", "ctx", "mp"),
    )
    out_specs = (P("section", "ctx", "mp"), P("section", "ctx", "mp"))
    return jax.shard_map(body, mesh=mesh, in_specs=in_specs, out_specs=out_specs, check_vma=False)
```

```python
import functools

import jax
import jax.numpy as jnp
from jax import lax
from jax.experimental import pallas as pl
from jax.experimental.pallas import tpu as pltpu
from jax.sharding import PartitionSpec as P

HEAD_DIM = 64
MESH = pl.DeviceIdType.MESH
NT = (((1,), (1,)), ((), ()))


def dot(a, b, dims=(((1,), (0,)), ((), ()))):
    return lax.dot_general(a, b, dims, preferred_element_type=jnp.float32)


def relay_kernel(
    n,
    order,
    q_hbm,
    k_hbm,
    v_hbm,
    w_hbm,
    hid_hbm,
    branch_out,
    hid_out,
    ctx_out,
    qkv,
    w,
    expo,
    total,
    ctx,
    part,
    red,
    zsrc,
    zin,
    local_sem,
    qkv_send,
    qkv_recv,
    hid_sem,
    ctx_send,
    ctx_recv,
    red_send,
    red_recv,
    z_send,
    z_recv,
    out_send,
    out_recv,
):
    s = lax.axis_index("section")
    c = lax.axis_index("ctx")
    m = lax.axis_index("mp")
    other = 1 - s
    wide = ctx.shape[2] // n
    rows = ctx.shape[1]
    depth = w_hbm.shape[0]
    cut = zsrc.shape[1]

    def columns(j):
        return pl.ds(pl.multiple_of(j * wide, wide), wide)

    def send(src, dst, send_sem, recv_sem, device):
        copy = pltpu.make_async_remote_copy(
            src_ref=src,
            dst_ref=dst,
            send_sem=send_sem,
            recv_sem=recv_sem,
            device_id=device,
            device_id_type=MESH,
        )
        copy.start()
        return copy

    inputs = (k_hbm, q_hbm, v_hbm)
    own = []
    for i, ref in enumerate(inputs):
        own.append(pltpu.make_async_copy(ref.at[:, columns(c)], qkv.at[i, c], local_sem.at[i]))
    own.append(pltpu.make_async_copy(w_hbm, w.at[pl.ds(0, depth)], local_sem.at[3]))
    for copy in own:
        copy.start()

    if n * cut > depth:
        w[depth:] = jnp.zeros((n * cut - depth, w.shape[1]), w.dtype)

    barrier = pltpu.get_barrier_semaphore()
    for d in range(1, n):
        pl.semaphore_signal(barrier, inc=1, device_id=(s, lax.rem(c + d, n), m), device_id_type=MESH)
        pl.semaphore_signal(barrier, inc=1, device_id=(s, c, lax.rem(m + d, n)), device_id_type=MESH)
    for a in range(n):
        pl.semaphore_signal(barrier, inc=1, device_id=(other, c, a), device_id_type=MESH)
    pl.semaphore_wait(barrier, 3 * n - 2)

    qkv_copies = []
    for i, ref in enumerate(inputs):
        group = []
        for d in range(1, n):
            j = lax.rem(c + d, n)
            group.append(
                send(ref.at[:, columns(j)], qkv.at[i, c], qkv_send.at[i, d - 1], qkv_recv.at[i, d - 1], (s, j, m))
            )
        qkv_copies.append(group)
    hid_copy = send(hid_hbm, hid_out, hid_sem.at[0], hid_sem.at[1], (other, c, m))

    lane = lax.broadcasted_iota(jnp.int32, (rows, wide), 1) // HEAD_DIM
    heads = wide // HEAD_DIM
    masks = [jnp.where(lane == h, 1.0, 0.0).astype(jnp.bfloat16) for h in range(heads)]
    for i in (0, 1):
        own[i].wait()
        for copy in qkv_copies[i]:
            copy.wait_recv()
    keys_all = qkv[0].reshape(n * rows, wide)
    for r in order:
        q_r = qkv[1, r]
        scores = dot(jnp.concatenate([q_r * mask for mask in masks], axis=0), keys_all, NT)
        e = jnp.exp(scores - jnp.max(scores, axis=1, keepdims=True))
        sums = jnp.sum(e, axis=1, keepdims=True)
        wide_sum = jnp.broadcast_to(sums[:rows], (rows, wide))
        for h in range(1, heads):
            wide_sum = jnp.where(lane == h, sums[h * rows : (h + 1) * rows], wide_sum)
        total[r] = wide_sum
        expo[r] = e.astype(jnp.bfloat16)

    own[2].wait()
    for copy in qkv_copies[2]:
        copy.wait_recv()
    values_all = qkv[2].reshape(n * rows, wide)

    relayed = (n - 1) * (2 - c)

    def ctx_copy(r, source, target, slot):
        return pltpu.make_async_remote_copy(
            src_ref=ctx.at[r, :, columns(source)],
            dst_ref=ctx.at[r, :, columns(source)],
            send_sem=ctx_send.at[r, slot],
            recv_sem=ctx_recv.at[r, source],
            device_id=(s, target, m),
            device_id_type=MESH,
        )

    def ctx_peers():
        for d in range(1, n):
            j = lax.rem(c + d, n)
            yield d - 1, j, jnp.abs(j - c) < n - 1

    def when(condition, action):
        @pl.when(condition)
        def _():
            action()

    def attend(r):
        both = dot(expo[r], values_all)
        picked = both[:rows]
        for h in range(1, heads):
            picked = jnp.where(lane == h, both[h * rows : (h + 1) * rows], picked)
        ctx[r, :, columns(c)] = (picked / total[r]).astype(jnp.bfloat16)
        for slot, j, direct in ctx_peers():
            when(direct, lambda: ctx_copy(r, c, j, slot).start())

    def ctx_arrive(r):
        @pl.when((c > 0) & (c < n - 1))
        def _():
            passing = ctx_copy(r, relayed, n - 1 - relayed, n - 1)
            passing.wait_recv()
            passing.start()

        for _, j, _ in ctx_peers():
            when(j != relayed, lambda: ctx_copy(r, j, j, 0).wait_recv())

    def ctx_sent(r):
        for slot, j, direct in ctx_peers():
            when(direct, lambda: ctx_copy(r, c, j, slot).wait_send())
        when((c > 0) & (c < n - 1), lambda: ctx_copy(r, relayed, n - 1 - relayed, n - 1).wait_send())

    red_copies = {}

    def project(r):
        ctx_arrive(r)
        part[r] = dot(w[...], ctx[r], NT).astype(jnp.bfloat16).reshape(part.shape[1:])
        group = []
        for d in range(1, n):
            t = lax.rem(m + d, n)
            group.append(
                send(part.at[r, t], red.at[r, d - 1], red_send.at[r, d - 1], red_recv.at[r, d - 1], (s, c, t))
            )
        red_copies[r] = group

    def z_copy(r):
        return pltpu.make_async_remote_copy(
            src_ref=zsrc.at[r],
            dst_ref=zin.at[c],
            send_sem=z_send.at[r],
            recv_sem=z_recv.at[c],
            device_id=(s, r, m),
            device_id_type=MESH,
        )

    def reduce(r):
        for copy in red_copies[r]:
            copy.wait_recv()
        acc = part[r, m].astype(jnp.float32)
        for d in range(1, n):
            acc = acc + red[r, d - 1].astype(jnp.float32)
        acc = acc.astype(jnp.bfloat16)

        @pl.when(c == r)
        def _():
            zin[c] = acc

        @pl.when(c != r)
        def _():
            zsrc[r] = acc
            z_copy(r).start()

    attend(order[0])
    own[3].wait()
    for i in range(n):
        if i < n - 1:
            attend(order[i + 1])
        project(order[i])
        if i > 1:
            reduce(order[i - 2])
    ctx_back = pltpu.make_async_copy(ctx.at[c], ctx_out, local_sem.at[4])
    ctx_back.start()
    for r in order[-2:]:
        reduce(r)

    out_copies = []
    for step in range(n):
        a = lax.rem(c + step, n)
        if step:
            pltpu.make_async_remote_copy(
                src_ref=zsrc.at[0],
                dst_ref=zin.at[a],
                send_sem=z_send.at[0],
                recv_sem=z_recv.at[a],
                device_id=(s, a, m),
                device_id_type=MESH,
            ).wait_recv()
        out_copies.append(
            send(
                zin.at[a],
                branch_out.at[pl.ds(pl.multiple_of(m * cut, cut), cut)],
                out_send.at[step],
                out_recv.at[m],
                (other, c, a),
            )
        )

    ctx_back.wait()
    for group in qkv_copies + list(red_copies.values()):
        for copy in group:
            copy.wait_send()
    hid_copy.wait()
    for r in range(n):
        ctx_sent(r)
        pl.when(c != r)(z_copy(r).wait_send)
    for copy in out_copies:
        copy.wait_send()
    for g in range(n):
        pltpu.make_async_remote_copy(
            src_ref=zin.at[0],
            dst_ref=branch_out.at[pl.ds(g * cut, cut)],
            send_sem=out_send.at[0],
            recv_sem=out_recv.at[g],
            device_id=(other, c, g),
            device_id_type=MESH,
        ).wait_recv()


def relay_body(n, hidden, query, keys, values, w_out):
    rows, inner = query.shape[1:]
    depth = hidden.shape[2]
    wide = inner // n
    heads = wide // HEAD_DIM
    cut = -(-depth // (16 * n)) * 16
    order = sorted(range(n), key=lambda r: (-abs(2 * r - n + 1), r))
    bf16 = jnp.bfloat16
    dma = pltpu.SemaphoreType.DMA
    hbm = pl.BlockSpec(memory_space=pltpu.HBM)
    branch, carried, context = pl.pallas_call(
        functools.partial(relay_kernel, n, order),
        out_shape=(
            jax.ShapeDtypeStruct((n * cut, rows), bf16),
            jax.ShapeDtypeStruct((depth, rows), bf16),
            jax.ShapeDtypeStruct((rows, inner), bf16),
        ),
        in_specs=[hbm] * 5,
        out_specs=(hbm,) * 3,
        scratch_shapes=[
            pltpu.VMEM((3, n, rows, wide), bf16),
            pltpu.VMEM((n * cut, inner), bf16),
            pltpu.VMEM((n, heads * rows, n * rows), bf16),
            pltpu.VMEM((n, rows, wide), jnp.float32),
            pltpu.VMEM((n, rows, inner), bf16),
            pltpu.VMEM((n, n, cut, rows), bf16),
            pltpu.VMEM((n, n - 1, cut, rows), bf16),
            pltpu.VMEM((n, cut, rows), bf16),
            pltpu.VMEM((n, cut, rows), bf16),
            dma((5,)),
            dma((3, n - 1)),
            dma((3, n - 1)),
            dma((2,)),
            dma((n, n)),
            dma((n, n)),
            dma((n, n - 1)),
            dma((n, n - 1)),
            dma((n,)),
            dma((n,)),
            dma((n,)),
            dma((n,)),
        ],
        compiler_params=pltpu.CompilerParams(
            collective_id=0, has_side_effects=True, vmem_limit_bytes=60 * 2**20
        ),
    )(query[0], keys[0], values[0], w_out[0], hidden[0].T)
    handed = (carried.astype(jnp.float32) + branch[:depth].astype(jnp.float32)).astype(bf16)
    return (handed.T[None], context[None])


def from_behind(block, axis, distance):
    devices = range(lax.axis_size(axis))
    route = [((i - distance) % len(devices), i) for i in devices]
    return lax.ppermute(block, axis, route)


def head_scores(query_h, keys_h):
    return jnp.einsum("qd,kd->qk", query_h, keys_h, preferred_element_type=jnp.float32)


def body(hidden, query, keys, values, w_out):
    n = lax.axis_size("ctx")
    square = lax.axis_size("mp") == n and lax.axis_size("section") == 2
    if square and n == 4 and query.shape[2] % (128 * n) == 0 and query.shape[1] % 128 == 0:
        return relay_body(n, hidden, query, keys, values, w_out)
    rows = hidden[0]
    query_rows = query[0]
    inner_dev = query_rows.shape[1]
    heads_dev = inner_dev // HEAD_DIM
    keys_local = keys[0]
    values_local = values[0]
    keys_all, values_all = (
        lax.all_gather(keys_local, "ctx", axis=0, tiled=True),
        lax.all_gather(values_local, "ctx", axis=0, tiled=True),
    )
    pieces = []
    for head in range(heads_dev):
        lower = head * HEAD_DIM
        upper = lower + HEAD_DIM
        scores = head_scores(query_rows[:, lower:upper], keys_all[:, lower:upper])
        peak = jnp.max(scores, axis=1, keepdims=True)
        expo = jnp.exp(scores - peak)
        total = jnp.sum(expo, axis=1, keepdims=True)
        summed = jnp.dot(
            expo.astype(jnp.bfloat16),
            values_all[:, lower:upper],
            preferred_element_type=jnp.float32,
        )
        pieces.append(summed / total)
    context = jnp.concatenate(pieces, axis=1).astype(jnp.bfloat16)
    out_local = w_out[0]
    context_all = lax.all_gather(context, "ctx", axis=0, tiled=True)
    projected = jnp.einsum(
        "ri,di->rd", context_all, out_local, preferred_element_type=jnp.float32
    ).astype(jnp.bfloat16)
    branch_terms = lax.all_to_all(projected, "ctx", split_axis=0, concat_axis=1, tiled=True).astype(
        jnp.float32
    )
    branch = lax.psum_scatter(
        branch_terms.astype(jnp.bfloat16), "mp", scatter_dimension=1, tiled=True
    ).astype(jnp.float32)
    result = (rows.astype(jnp.float32) + branch).astype(jnp.bfloat16)
    handed = from_behind(result, "section", 1)
    return (handed[None], context[None])


def solution(mesh):
    in_specs = (
        P("section", "ctx", "mp"),
        P("section", "ctx", "mp"),
        P("section", "ctx", "mp"),
        P("section", "ctx", "mp"),
        P("section", "ctx", "mp"),
    )
    out_specs = (P("section", "ctx", "mp"), P("section", "ctx", "mp"))
    return jax.shard_map(body, mesh=mesh, in_specs=in_specs, out_specs=out_specs, check_vma=False)
```

```python
import functools

import jax
import jax.numpy as jnp
from jax import lax
from jax.experimental import pallas as pl
from jax.experimental.pallas import tpu as pltpu
from jax.sharding import PartitionSpec as P

HEAD_DIM = 64
MESH = pl.DeviceIdType.MESH
NT = (((1,), (1,)), ((), ()))


def dot(a, b, dims=(((1,), (0,)), ((), ()))):
    return lax.dot_general(a, b, dims, preferred_element_type=jnp.float32)


def relay_kernel(
    n,
    shifts,
    q_hbm,
    k_hbm,
    v_hbm,
    w_hbm,
    hid_hbm,
    branch_out,
    hid_out,
    ctx_out,
    qkv,
    w,
    expo,
    total,
    ctx,
    part,
    red,
    zsrc,
    zin,
    local_sem,
    qkv_send,
    qkv_recv,
    hid_sem,
    ctx_send,
    ctx_recv,
    red_send,
    red_recv,
    z_send,
    z_recv,
    out_send,
    out_recv,
):
    s = lax.axis_index("section")
    c = lax.axis_index("ctx")
    m = lax.axis_index("mp")
    other = 1 - s
    wide = ctx.shape[2] // n
    rows = ctx.shape[1]
    depth = w_hbm.shape[0]
    cut = zsrc.shape[1]

    def columns(j):
        return pl.ds(pl.multiple_of(j * wide, wide), wide)

    def send(src, dst, send_sem, recv_sem, device):
        copy = pltpu.make_async_remote_copy(
            src_ref=src,
            dst_ref=dst,
            send_sem=send_sem,
            recv_sem=recv_sem,
            device_id=device,
            device_id_type=MESH,
        )
        copy.start()
        return copy

    inputs = (k_hbm, q_hbm, v_hbm)
    own = []
    for i, ref in enumerate(inputs):
        own.append(pltpu.make_async_copy(ref.at[:, columns(c)], qkv.at[i, c], local_sem.at[i]))
    own.append(pltpu.make_async_copy(w_hbm, w.at[pl.ds(0, depth)], local_sem.at[3]))
    for copy in own:
        copy.start()

    if n * cut > depth:
        w[depth:] = jnp.zeros((n * cut - depth, w.shape[1]), w.dtype)

    barrier = pltpu.get_barrier_semaphore()
    for d in range(1, n):
        pl.semaphore_signal(barrier, inc=1, device_id=(s, lax.rem(c + d, n), m), device_id_type=MESH)
        pl.semaphore_signal(barrier, inc=1, device_id=(s, c, lax.rem(m + d, n)), device_id_type=MESH)
    for a in range(n):
        pl.semaphore_signal(barrier, inc=1, device_id=(other, c, a), device_id_type=MESH)
    pl.semaphore_wait(barrier, 3 * n - 2)

    qkv_copies = []
    for i, ref in enumerate(inputs):
        group = []
        for d in range(1, n):
            j = lax.rem(c + d, n)
            group.append(
                send(ref.at[:, columns(j)], qkv.at[i, c], qkv_send.at[i, d - 1], qkv_recv.at[i, d - 1], (s, j, m))
            )
        qkv_copies.append(group)
    hid_copy = send(hid_hbm, hid_out, hid_sem.at[0], hid_sem.at[1], (other, c, m))

    lane = lax.broadcasted_iota(jnp.int32, (rows, wide), 1) // HEAD_DIM
    heads = wide // HEAD_DIM
    masks = [jnp.where(lane == h, 1.0, 0.0).astype(jnp.bfloat16) for h in range(heads)]
    for i in (0, 1):
        own[i].wait()
        for copy in qkv_copies[i]:
            copy.wait_recv()

    @pl.loop(0, n)
    def _(r):
        keys_all = qkv[0].reshape(n * rows, wide)
        q_r = qkv[1, r]
        scores = dot(jnp.concatenate([q_r * mask for mask in masks], axis=0), keys_all, NT)
        e = jnp.exp(scores - jnp.max(scores, axis=1, keepdims=True))
        sums = jnp.sum(e, axis=1, keepdims=True)
        wide_sum = jnp.broadcast_to(sums[:rows], (rows, wide))
        for h in range(1, heads):
            wide_sum = jnp.where(lane == h, sums[h * rows : (h + 1) * rows], wide_sum)
        total[r] = wide_sum
        expo[r] = e.astype(jnp.bfloat16)

    own[2].wait()
    for copy in qkv_copies[2]:
        copy.wait_recv()

    @pl.loop(0, n)
    def _(r):
        values_all = qkv[2].reshape(n * rows, wide)
        both = dot(expo[r], values_all)
        picked = both[:rows]
        for h in range(1, heads):
            picked = jnp.where(lane == h, both[h * rows : (h + 1) * rows], picked)
        ctx[r, :, columns(c)] = (picked / total[r]).astype(jnp.bfloat16)

    def share(i):
        group = []
        for d in range(1, n):
            j = lax.rem(c + d, n)
            block = ctx.at[lax.rem(j + shifts[i], n), :, columns(c)]
            group.append(send(block, block, ctx_send.at[i, d - 1], ctx_recv.at[i, d - 1], (s, j, m)))
        ctx_copies.append(group)

    ctx_copies = []
    share(0)
    share(1)
    own[3].wait()
    red_copies = []

    def project(i):
        for d in range(1, n):
            block = ctx.at[lax.rem(c + shifts[i], n), :, columns(lax.rem(c + d, n))]
            pltpu.make_async_remote_copy(
                src_ref=block,
                dst_ref=block,
                send_sem=ctx_send.at[i, d - 1],
                recv_sem=ctx_recv.at[i, n - 1 - d],
                device_id=(s, lax.rem(c + d, n), m),
                device_id_type=MESH,
            ).wait_recv()
        r = lax.rem(c + shifts[i], n)
        part[i] = dot(w[...], ctx[r], NT).astype(jnp.bfloat16).reshape(part.shape[1:])
        group = []
        for d in range(1, n):
            t = lax.rem(m + d, n)
            group.append(
                send(part.at[i, t], red.at[i, d - 1], red_send.at[i, d - 1], red_recv.at[i, d - 1], (s, c, t))
            )
        red_copies.append(group)

    z_copies = []

    def reduce(i):
        for copy in red_copies[i]:
            copy.wait_recv()
        acc = part[i, m].astype(jnp.float32)
        for d in range(1, n):
            acc = acc + red[i, d - 1].astype(jnp.float32)
        if shifts[i] == 0:
            zin[i] = acc.astype(jnp.bfloat16)
        else:
            zsrc[i] = acc.astype(jnp.bfloat16)
            target = lax.rem(c + shifts[i], n)
            z_copies.append(send(zsrc.at[i], zin.at[i], z_send.at[i], z_recv.at[i], (s, target, m)))

    out_copies = []

    def hand_over(i):
        if shifts[i]:
            z_copies[i].wait_recv()
        target = lax.rem(c + n - shifts[i], n)
        piece = branch_out.at[pl.ds(pl.multiple_of(m * cut, cut), cut)]
        out_copies.append(send(zin.at[i], piece, out_send.at[i], out_recv.at[m], (other, c, target)))

    project(0)
    for i in range(2, n):
        share(i)
        project(i - 1)
        if i > 2:
            reduce(i - 3)
    project(n - 1)
    ctx_back = pltpu.make_async_copy(ctx.at[c], ctx_out, local_sem.at[4])
    ctx_back.start()
    for i in range(n - 3, n):
        reduce(i)
        if i < n - 1:
            hand_over(i - 1)
    hand_over(n - 1)
    hand_over(n - 2)

    ctx_back.wait()
    for group in qkv_copies + ctx_copies + red_copies + [z_copies, out_copies]:
        for copy in group:
            copy.wait_send()
    hid_copy.wait()
    for g in range(n):
        pltpu.make_async_remote_copy(
            src_ref=zin.at[0],
            dst_ref=branch_out.at[pl.ds(g * cut, cut)],
            send_sem=out_send.at[0],
            recv_sem=out_recv.at[g],
            device_id=(other, c, g),
            device_id_type=MESH,
        ).wait_recv()


def relay_body(n, hidden, query, keys, values, w_out):
    rows, inner = query.shape[1:]
    depth = hidden.shape[2]
    wide = inner // n
    heads = wide // HEAD_DIM
    cut = -(-depth // (16 * n)) * 16
    bf16 = jnp.bfloat16
    dma = pltpu.SemaphoreType.DMA
    hbm = pl.BlockSpec(memory_space=pltpu.HBM)
    branch, carried, context = pl.pallas_call(
        functools.partial(relay_kernel, n, (2, 1, 3, 0)),
        out_shape=(
            jax.ShapeDtypeStruct((n * cut, rows), bf16),
            jax.ShapeDtypeStruct((depth, rows), bf16),
            jax.ShapeDtypeStruct((rows, inner), bf16),
        ),
        in_specs=[hbm] * 5,
        out_specs=(hbm,) * 3,
        scratch_shapes=[
            pltpu.VMEM((3, n, rows, wide), bf16),
            pltpu.VMEM((n * cut, inner), bf16),
            pltpu.VMEM((n, heads * rows, n * rows), bf16),
            pltpu.VMEM((n, rows, wide), jnp.float32),
            pltpu.VMEM((n, rows, inner), bf16),
            pltpu.VMEM((n, n, cut, rows), bf16),
            pltpu.VMEM((n, n - 1, cut, rows), bf16),
            pltpu.VMEM((n, cut, rows), bf16),
            pltpu.VMEM((n, cut, rows), bf16),
            dma((5,)),
            dma((3, n - 1)),
            dma((3, n - 1)),
            dma((2,)),
            dma((n, n - 1)),
            dma((n, n - 1)),
            dma((n, n - 1)),
            dma((n, n - 1)),
            dma((n,)),
            dma((n,)),
            dma((n,)),
            dma((n,)),
        ],
        compiler_params=pltpu.CompilerParams(
            collective_id=0, has_side_effects=True, vmem_limit_bytes=60 * 2**20
        ),
    )(query[0], keys[0], values[0], w_out[0], hidden[0].T)
    handed, context = pl.pallas_call(
        finish_kernel,
        out_shape=(
            jax.ShapeDtypeStruct((depth, rows), bf16),
            jax.ShapeDtypeStruct((rows, inner), bf16),
        ),
        in_specs=[hbm] * 3,
        out_specs=(hbm,) * 2,
        scratch_shapes=[pltpu.VMEM((depth, rows), bf16)] * 3 + [dma((4,))],
        compiler_params=pltpu.CompilerParams(vmem_limit_bytes=60 * 2**20),
    )(carried, branch, context)
    return (handed.T[None], context[None])


def finish_kernel(carried, branch, context, handed, context_out, first, second, summed, sem):
    depth = handed.shape[0]
    kept = pltpu.make_async_copy(context, context_out, sem.at[0])
    one = pltpu.make_async_copy(carried, first, sem.at[1])
    two = pltpu.make_async_copy(branch.at[pl.ds(0, depth)], second, sem.at[2])
    for copy in (one, two, kept):
        copy.start()
    one.wait()
    two.wait()
    summed[...] = (first[...].astype(jnp.float32) + second[...].astype(jnp.float32)).astype(jnp.bfloat16)
    last = pltpu.make_async_copy(summed, handed, sem.at[3])
    last.start()
    last.wait()
    kept.wait()


def from_behind(block, axis, distance):
    devices = range(lax.axis_size(axis))
    route = [((i - distance) % len(devices), i) for i in devices]
    return lax.ppermute(block, axis, route)


def head_scores(query_h, keys_h):
    return jnp.einsum("qd,kd->qk", query_h, keys_h, preferred_element_type=jnp.float32)


def body(hidden, query, keys, values, w_out):
    n = lax.axis_size("ctx")
    square = lax.axis_size("mp") == n and lax.axis_size("section") == 2
    if square and n == 4 and query.shape[2] % (128 * n) == 0 and query.shape[1] % 128 == 0:
        return relay_body(n, hidden, query, keys, values, w_out)
    rows = hidden[0]
    query_rows = query[0]
    inner_dev = query_rows.shape[1]
    heads_dev = inner_dev // HEAD_DIM
    keys_local = keys[0]
    values_local = values[0]
    keys_all, values_all = (
        lax.all_gather(keys_local, "ctx", axis=0, tiled=True),
        lax.all_gather(values_local, "ctx", axis=0, tiled=True),
    )
    pieces = []
    for head in range(heads_dev):
        lower = head * HEAD_DIM
        upper = lower + HEAD_DIM
        scores = head_scores(query_rows[:, lower:upper], keys_all[:, lower:upper])
        peak = jnp.max(scores, axis=1, keepdims=True)
        expo = jnp.exp(scores - peak)
        total = jnp.sum(expo, axis=1, keepdims=True)
        summed = jnp.dot(
            expo.astype(jnp.bfloat16),
            values_all[:, lower:upper],
            preferred_element_type=jnp.float32,
        )
        pieces.append(summed / total)
    context = jnp.concatenate(pieces, axis=1).astype(jnp.bfloat16)
    out_local = w_out[0]
    context_all = lax.all_gather(context, "ctx", axis=0, tiled=True)
    projected = jnp.einsum(
        "ri,di->rd", context_all, out_local, preferred_element_type=jnp.float32
    ).astype(jnp.bfloat16)
    branch_terms = lax.all_to_all(projected, "ctx", split_axis=0, concat_axis=1, tiled=True).astype(
        jnp.float32
    )
    branch = lax.psum_scatter(
        branch_terms.astype(jnp.bfloat16), "mp", scatter_dimension=1, tiled=True
    ).astype(jnp.float32)
    result = (rows.astype(jnp.float32) + branch).astype(jnp.bfloat16)
    handed = from_behind(result, "section", 1)
    return (handed[None], context[None])


def solution(mesh):
    in_specs = (
        P("section", "ctx", "mp"),
        P("section", "ctx", "mp"),
        P("section", "ctx", "mp"),
        P("section", "ctx", "mp"),
        P("section", "ctx", "mp"),
    )
    out_specs = (P("section", "ctx", "mp"), P("section", "ctx", "mp"))
    return jax.shard_map(body, mesh=mesh, in_specs=in_specs, out_specs=out_specs, check_vma=False)
```

```python
import functools

import jax
import jax.numpy as jnp
from jax import lax
from jax.experimental import pallas as pl
from jax.experimental.pallas import tpu as pltpu
from jax.sharding import PartitionSpec as P

HEAD_DIM = 64
MESH = pl.DeviceIdType.MESH
NT = (((1,), (1,)), ((), ()))


def dot(a, b, dims=(((1,), (0,)), ((), ()))):
    return lax.dot_general(a, b, dims, preferred_element_type=jnp.float32)


def relay_kernel(
    n,
    shifts,
    q_hbm,
    k_hbm,
    v_hbm,
    w_hbm,
    hid_hbm,
    branch_out,
    hid_out,
    ctx_out,
    staged,
    hid,
    qkv,
    w,
    expo,
    total,
    ctx,
    part,
    red,
    zsrc,
    zin,
    local_sem,
    qkv_send,
    qkv_recv,
    hid_sem,
    ctx_send,
    ctx_recv,
    red_send,
    red_recv,
    z_send,
    z_recv,
    out_send,
    out_recv,
):
    s = lax.axis_index("section")
    c = lax.axis_index("ctx")
    m = lax.axis_index("mp")
    other = 1 - s
    wide = ctx.shape[2] // n
    rows = ctx.shape[1]
    depth = w_hbm.shape[0]
    cut = zsrc.shape[1]

    def columns(j):
        return pl.ds(pl.multiple_of(j * wide, wide), wide)

    def send(src, dst, send_sem, recv_sem, device):
        copy = pltpu.make_async_remote_copy(
            src_ref=src,
            dst_ref=dst,
            send_sem=send_sem,
            recv_sem=recv_sem,
            device_id=device,
            device_id_type=MESH,
        )
        copy.start()
        return copy

    inputs = (k_hbm, q_hbm, v_hbm)
    own = [pltpu.make_async_copy(ref, staged.at[i], local_sem.at[i]) for i, ref in enumerate(inputs)]
    own.append(pltpu.make_async_copy(w_hbm, w.at[pl.ds(0, depth)], local_sem.at[3]))
    own.append(pltpu.make_async_copy(hid_hbm, hid, local_sem.at[4]))
    for copy in own:
        copy.start()

    if n * cut > depth:
        w[depth:] = jnp.zeros((n * cut - depth, w.shape[1]), w.dtype)

    barrier = pltpu.get_barrier_semaphore()
    for d in range(1, n):
        pl.semaphore_signal(barrier, inc=1, device_id=(s, lax.rem(c + d, n), m), device_id_type=MESH)
        pl.semaphore_signal(barrier, inc=1, device_id=(s, c, lax.rem(m + d, n)), device_id_type=MESH)
    for a in range(n):
        pl.semaphore_signal(barrier, inc=1, device_id=(other, c, a), device_id_type=MESH)
    pl.semaphore_wait(barrier, 3 * n - 2)

    qkv_copies = []
    for i in range(3):
        own[i].wait()
        group = []
        for d in range(1, n):
            j = lax.rem(c + d, n)
            group.append(
                send(staged.at[i, :, columns(j)], qkv.at[i, c], qkv_send.at[i, d - 1], qkv_recv.at[i, d - 1], (s, j, m))
            )
        qkv_copies.append(group)
    for i in range(3):
        qkv[i, c] = staged[i, :, columns(c)]

    lane = lax.broadcasted_iota(jnp.int32, (rows, wide), 1) // HEAD_DIM
    heads = wide // HEAD_DIM
    masks = [jnp.where(lane == h, 1.0, 0.0).astype(jnp.bfloat16) for h in range(heads)]
    for i in (0, 1):
        for copy in qkv_copies[i]:
            copy.wait_recv()

    @pl.loop(0, n)
    def _(r):
        keys_all = qkv[0].reshape(n * rows, wide)
        q_r = qkv[1, r]
        scores = dot(jnp.concatenate([q_r * mask for mask in masks], axis=0), keys_all, NT)
        e = jnp.exp(scores - jnp.max(scores, axis=1, keepdims=True))
        sums = jnp.sum(e, axis=1, keepdims=True)
        wide_sum = jnp.broadcast_to(sums[:rows], (rows, wide))
        for h in range(1, heads):
            wide_sum = jnp.where(lane == h, sums[h * rows : (h + 1) * rows], wide_sum)
        total[r] = wide_sum
        expo[r] = e.astype(jnp.bfloat16)

    for copy in qkv_copies[2]:
        copy.wait_recv()

    @pl.loop(0, n)
    def _(r):
        values_all = qkv[2].reshape(n * rows, wide)
        both = dot(expo[r], values_all)
        picked = both[:rows]
        for h in range(1, heads):
            picked = jnp.where(lane == h, both[h * rows : (h + 1) * rows], picked)
        ctx[r, :, columns(c)] = (picked / total[r]).astype(jnp.bfloat16)

    def share(i):
        group = []
        for d in range(1, n):
            j = lax.rem(c + d, n)
            block = ctx.at[lax.rem(j + shifts[i], n), :, columns(c)]
            group.append(send(block, block, ctx_send.at[i, d - 1], ctx_recv.at[i, d - 1], (s, j, m)))
        ctx_copies.append(group)

    ctx_copies = []
    share(0)
    share(1)
    own[4].wait()
    hid_copy = send(hid, hid_out, hid_sem.at[0], hid_sem.at[1], (other, c, m))
    own[3].wait()

    def red_copy(i, d):
        t = lax.rem(m + d, n)
        return pltpu.make_async_remote_copy(
            src_ref=part.at[i, t],
            dst_ref=red.at[i, d - 1],
            send_sem=red_send.at[i, d - 1],
            recv_sem=red_recv.at[i, d - 1],
            device_id=(s, c, t),
            device_id_type=MESH,
        )

    def project(i):
        for d in range(1, n):
            block = ctx.at[lax.rem(c + shifts[i], n), :, columns(lax.rem(c + d, n))]
            pltpu.make_async_remote_copy(
                src_ref=block,
                dst_ref=block,
                send_sem=ctx_send.at[i, d - 1],
                recv_sem=ctx_recv.at[i, n - 1 - d],
                device_id=(s, lax.rem(c + d, n), m),
                device_id_type=MESH,
            ).wait_recv()
        r = lax.rem(c + shifts[i], n)

        @pl.loop(1, n + 1)
        def _(d):
            t = lax.rem(m + d, n)
            piece = w[pl.ds(pl.multiple_of(t * cut, cut), cut), :]
            part[i, t] = dot(piece, ctx[r], NT).astype(jnp.bfloat16)

            @pl.when(d < n)
            def _():
                red_copy(i, d).start()

    z_copies = []

    def reduce(i):
        for d in range(1, n):
            red_copy(i, d).wait_recv()
        acc = part[i, m].astype(jnp.float32)
        for d in range(1, n):
            acc = acc + red[i, d - 1].astype(jnp.float32)
        if shifts[i] == 0:
            zin[i] = acc.astype(jnp.bfloat16)
        else:
            zsrc[i] = acc.astype(jnp.bfloat16)
            target = lax.rem(c + shifts[i], n)
            z_copies.append(send(zsrc.at[i], zin.at[i], z_send.at[i], z_recv.at[i], (s, target, m)))

    out_copies = []

    def hand_over(i):
        if shifts[i]:
            z_copies[i].wait_recv()
        target = lax.rem(c + n - shifts[i], n)
        piece = branch_out.at[pl.ds(pl.multiple_of(m * cut, cut), cut)]
        out_copies.append(send(zin.at[i], piece, out_send.at[i], out_recv.at[m], (other, c, target)))

    project(0)
    for i in range(2, n):
        share(i)
        project(i - 1)
        if i > 2:
            reduce(i - 3)
    project(n - 1)
    ctx_back = pltpu.make_async_copy(ctx.at[c], ctx_out, local_sem.at[5])
    ctx_back.start()
    for i in range(n - 3, n):
        reduce(i)
        if i < n - 1:
            hand_over(i - 1)
    hand_over(n - 1)
    hand_over(n - 2)

    ctx_back.wait()
    for group in qkv_copies + ctx_copies + [z_copies, out_copies]:
        for copy in group:
            copy.wait_send()
    hid_copy.wait()
    for i in range(n):
        for d in range(1, n):
            red_copy(i, d).wait_send()
    for g in range(n):
        pltpu.make_async_remote_copy(
            src_ref=zin.at[0],
            dst_ref=branch_out.at[pl.ds(g * cut, cut)],
            send_sem=out_send.at[0],
            recv_sem=out_recv.at[g],
            device_id=(other, c, g),
            device_id_type=MESH,
        ).wait_recv()


def relay_body(n, hidden, query, keys, values, w_out):
    rows, inner = query.shape[1:]
    depth = hidden.shape[2]
    wide = inner // n
    heads = wide // HEAD_DIM
    cut = -(-depth // (16 * n)) * 16
    bf16 = jnp.bfloat16
    dma = pltpu.SemaphoreType.DMA
    hbm = pl.BlockSpec(memory_space=pltpu.HBM)
    branch, carried, context = pl.pallas_call(
        functools.partial(relay_kernel, n, (2, 1, 3, 0)),
        out_shape=(
            jax.ShapeDtypeStruct((n * cut, rows), bf16),
            jax.ShapeDtypeStruct((depth, rows), bf16),
            jax.ShapeDtypeStruct((rows, inner), bf16),
        ),
        in_specs=[hbm] * 5,
        out_specs=(hbm,) * 3,
        scratch_shapes=[
            pltpu.VMEM((3, rows, inner), bf16),
            pltpu.VMEM((depth, rows), bf16),
            pltpu.VMEM((3, n, rows, wide), bf16),
            pltpu.VMEM((n * cut, inner), bf16),
            pltpu.VMEM((n, heads * rows, n * rows), bf16),
            pltpu.VMEM((n, rows, wide), jnp.float32),
            pltpu.VMEM((n, rows, inner), bf16),
            pltpu.VMEM((n, n, cut, rows), bf16),
            pltpu.VMEM((n, n - 1, cut, rows), bf16),
            pltpu.VMEM((n, cut, rows), bf16),
            pltpu.VMEM((n, cut, rows), bf16),
            dma((6,)),
            dma((3, n - 1)),
            dma((3, n - 1)),
            dma((2,)),
            dma((n, n - 1)),
            dma((n, n - 1)),
            dma((n, n - 1)),
            dma((n, n - 1)),
            dma((n,)),
            dma((n,)),
            dma((n,)),
            dma((n,)),
        ],
        compiler_params=pltpu.CompilerParams(
            collective_id=0, has_side_effects=True, vmem_limit_bytes=60 * 2**20
        ),
    )(query[0], keys[0], values[0], w_out[0], hidden[0].T)
    handed, context = pl.pallas_call(
        finish_kernel,
        out_shape=(
            jax.ShapeDtypeStruct((depth, rows), bf16),
            jax.ShapeDtypeStruct((rows, inner), bf16),
        ),
        in_specs=[hbm] * 3,
        out_specs=(hbm,) * 2,
        scratch_shapes=[pltpu.VMEM((depth, rows), bf16)] * 3 + [pltpu.VMEM((rows, inner), bf16), dma((5,))],
        compiler_params=pltpu.CompilerParams(vmem_limit_bytes=60 * 2**20),
    )(carried, branch, context)
    return (handed.T[None], context[None])


def finish_kernel(carried, branch, context, handed, context_out, first, second, summed, kept, sem):
    depth = handed.shape[0]
    one = pltpu.make_async_copy(carried, first, sem.at[0])
    two = pltpu.make_async_copy(branch.at[pl.ds(0, depth)], second, sem.at[1])
    three = pltpu.make_async_copy(context, kept, sem.at[2])
    for copy in (one, two, three):
        copy.start()
    three.wait()
    last = pltpu.make_async_copy(kept, context_out, sem.at[3])
    last.start()
    one.wait()
    two.wait()
    summed[...] = (first[...].astype(jnp.float32) + second[...].astype(jnp.float32)).astype(jnp.bfloat16)
    result = pltpu.make_async_copy(summed, handed, sem.at[4])
    result.start()
    last.wait()
    result.wait()


def from_behind(block, axis, distance):
    devices = range(lax.axis_size(axis))
    route = [((i - distance) % len(devices), i) for i in devices]
    return lax.ppermute(block, axis, route)


def head_scores(query_h, keys_h):
    return jnp.einsum("qd,kd->qk", query_h, keys_h, preferred_element_type=jnp.float32)


def body(hidden, query, keys, values, w_out):
    n = lax.axis_size("ctx")
    square = lax.axis_size("mp") == n and lax.axis_size("section") == 2
    if square and n == 4 and query.shape[2] % (128 * n) == 0 and query.shape[1] % 128 == 0:
        return relay_body(n, hidden, query, keys, values, w_out)
    rows = hidden[0]
    query_rows = query[0]
    inner_dev = query_rows.shape[1]
    heads_dev = inner_dev // HEAD_DIM
    keys_local = keys[0]
    values_local = values[0]
    keys_all, values_all = (
        lax.all_gather(keys_local, "ctx", axis=0, tiled=True),
        lax.all_gather(values_local, "ctx", axis=0, tiled=True),
    )
    pieces = []
    for head in range(heads_dev):
        lower = head * HEAD_DIM
        upper = lower + HEAD_DIM
        scores = head_scores(query_rows[:, lower:upper], keys_all[:, lower:upper])
        peak = jnp.max(scores, axis=1, keepdims=True)
        expo = jnp.exp(scores - peak)
        total = jnp.sum(expo, axis=1, keepdims=True)
        summed = jnp.dot(
            expo.astype(jnp.bfloat16),
            values_all[:, lower:upper],
            preferred_element_type=jnp.float32,
        )
        pieces.append(summed / total)
    context = jnp.concatenate(pieces, axis=1).astype(jnp.bfloat16)
    out_local = w_out[0]
    context_all = lax.all_gather(context, "ctx", axis=0, tiled=True)
    projected = jnp.einsum(
        "ri,di->rd", context_all, out_local, preferred_element_type=jnp.float32
    ).astype(jnp.bfloat16)
    branch_terms = lax.all_to_all(projected, "ctx", split_axis=0, concat_axis=1, tiled=True).astype(
        jnp.float32
    )
    branch = lax.psum_scatter(
        branch_terms.astype(jnp.bfloat16), "mp", scatter_dimension=1, tiled=True
    ).astype(jnp.float32)
    result = (rows.astype(jnp.float32) + branch).astype(jnp.bfloat16)
    handed = from_behind(result, "section", 1)
    return (handed[None], context[None])


def solution(mesh):
    in_specs = (
        P("section", "ctx", "mp"),
        P("section", "ctx", "mp"),
        P("section", "ctx", "mp"),
        P("section", "ctx", "mp"),
        P("section", "ctx", "mp"),
    )
    out_specs = (P("section", "ctx", "mp"), P("section", "ctx", "mp"))
    return jax.shard_map(body, mesh=mesh, in_specs=in_specs, out_specs=out_specs, check_vma=False)
```

```python
import functools

import jax
import jax.numpy as jnp
from jax import lax
from jax.experimental import pallas as pl
from jax.experimental.pallas import tpu as pltpu
from jax.sharding import PartitionSpec as P

HEAD_DIM = 64
MESH = pl.DeviceIdType.MESH
NT = (((1,), (1,)), ((), ()))


def dot(a, b, dims=(((1,), (0,)), ((), ()))):
    return lax.dot_general(a, b, dims, preferred_element_type=jnp.float32)


def relay_kernel(
    n,
    q_hbm,
    k_hbm,
    v_hbm,
    w_hbm,
    hid_hbm,
    branch_out,
    hid_out,
    ctx_out,
    staged,
    hid,
    qkv,
    w,
    expo,
    total,
    ctx,
    part,
    red,
    zsrc,
    zin,
    local_sem,
    qkv_send,
    qkv_recv,
    hid_sem,
    ctx_send,
    ctx_recv,
    red_send,
    red_recv,
    z_send,
    z_recv,
    out_send,
    out_recv,
):
    s = lax.axis_index("section")
    c = lax.axis_index("ctx")
    m = lax.axis_index("mp")
    other = 1 - s
    wide = ctx.shape[2] // n
    rows = ctx.shape[1]
    depth = w_hbm.shape[0]
    cut = zsrc.shape[1]

    def columns(j):
        return pl.ds(pl.multiple_of(j * wide, wide), wide)

    def send(src, dst, send_sem, recv_sem, device):
        copy = pltpu.make_async_remote_copy(
            src_ref=src,
            dst_ref=dst,
            send_sem=send_sem,
            recv_sem=recv_sem,
            device_id=device,
            device_id_type=MESH,
        )
        copy.start()
        return copy

    inputs = (k_hbm, q_hbm, v_hbm)
    own = [pltpu.make_async_copy(ref, staged.at[i], local_sem.at[i]) for i, ref in enumerate(inputs)]
    own.append(pltpu.make_async_copy(w_hbm, w.at[pl.ds(0, depth)], local_sem.at[3]))
    own.append(pltpu.make_async_copy(hid_hbm, hid, local_sem.at[4]))
    for copy in own:
        copy.start()

    if n * cut > depth:
        w[depth:] = jnp.zeros((n * cut - depth, w.shape[1]), w.dtype)

    barrier = pltpu.get_barrier_semaphore()
    for d in range(1, n):
        pl.semaphore_signal(barrier, inc=1, device_id=(s, lax.rem(c + d, n), m), device_id_type=MESH)
        pl.semaphore_signal(barrier, inc=1, device_id=(s, c, lax.rem(m + d, n)), device_id_type=MESH)
    for a in range(n):
        pl.semaphore_signal(barrier, inc=1, device_id=(other, c, a), device_id_type=MESH)
    pl.semaphore_wait(barrier, 3 * n - 2)

    qkv_copies = []
    for i in range(3):
        own[i].wait()
        group = []
        for d in range(1, n):
            j = lax.rem(c + d, n)
            group.append(
                send(staged.at[i, :, columns(j)], qkv.at[i, c], qkv_send.at[i, d - 1], qkv_recv.at[i, d - 1], (s, j, m))
            )
        qkv_copies.append(group)
    for i in range(3):
        qkv[i, c] = staged[i, :, columns(c)]

    lane = lax.broadcasted_iota(jnp.int32, (rows, wide), 1) // HEAD_DIM
    heads = wide // HEAD_DIM
    masks = [jnp.where(lane == h, 1.0, 0.0).astype(jnp.bfloat16) for h in range(heads)]
    for i in (0, 1):
        for copy in qkv_copies[i]:
            copy.wait_recv()

    @pl.loop(0, n)
    def _(r):
        keys_all = qkv[0].reshape(n * rows, wide)
        q_r = qkv[1, r]
        scores = dot(jnp.concatenate([q_r * mask for mask in masks], axis=0), keys_all, NT)
        e = jnp.exp(scores - jnp.max(scores, axis=1, keepdims=True))
        sums = jnp.sum(e, axis=1, keepdims=True)
        wide_sum = jnp.broadcast_to(sums[:rows], (rows, wide))
        for h in range(1, heads):
            wide_sum = jnp.where(lane == h, sums[h * rows : (h + 1) * rows], wide_sum)
        total[r] = wide_sum
        expo[r] = e.astype(jnp.bfloat16)

    for copy in qkv_copies[2]:
        copy.wait_recv()

    @pl.loop(0, n)
    def _(r):
        values_all = qkv[2].reshape(n * rows, wide)
        both = dot(expo[r], values_all)
        picked = both[:rows]
        for h in range(1, heads):
            picked = jnp.where(lane == h, both[h * rows : (h + 1) * rows], picked)
        ctx[r, :, columns(c)] = (picked / total[r]).astype(jnp.bfloat16)

    inner = (c == 1) | (c == 2)
    mate = c + 1 - 2 * lax.rem(c, 2)
    far = jnp.where(c < 2, 2, 0)
    far_inner = jnp.where(c < 2, 2, 1)

    def pair_block(plane, i):
        return jnp.where(plane < 2, n - 1 - i, i)

    def block_of(plane, i):
        if i < 2:
            return pair_block(plane, i)
        return pair_block(plane, jnp.where((plane == 1) | (plane == 2), 5 - i, i))

    def ctx_copy(block, kind, i, arrival, target):
        return pltpu.make_async_remote_copy(
            src_ref=block,
            dst_ref=block,
            send_sem=ctx_send.at[kind, i],
            recv_sem=ctx_recv.at[arrival, i],
            device_id=(s, target, m),
            device_id_type=MESH,
        )

    def when(condition, action):
        @pl.when(condition)
        def _():
            action()

    def to_mate(i):
        return ctx_copy(ctx.at[block_of(mate, i), :, columns(c)], 0, i, 0, mate)

    def to_far(i):
        block = ctx.at[pair_block(far_inner, i), :, columns(c)]
        return ctx_copy(block, 1, i, 1 + lax.rem(c, 2), far_inner)

    def relayed(i):
        both = pl.ds(pl.multiple_of(far * wide, wide), 2 * wide)
        return ctx_copy(ctx.at[pair_block(c, i), :, both], 2, i, 3, mate)

    def share(i):
        to_far(i).start()
        to_mate(i).start()

    def relay(i):
        for k in range(2):
            block = ctx.at[pair_block(c, i), :, columns(far + k)]
            ctx_copy(block, 1, i, 1 + k, far_inner).wait_recv()
        relayed(i).start()

    def arrive(i):
        for k in ((i,), (i,), (2, 3), ())[i]:
            when(inner, lambda: relay(k))
        when(~inner, lambda: relayed(i).wait_recv())
        ctx_copy(ctx.at[block_of(c, i), :, columns(mate)], 0, i, 0, mate).wait_recv()

    def ctx_sent(i):
        to_far(i).wait_send()
        to_mate(i).wait_send()
        when(inner, lambda: relayed(i).wait_send())

    share(0)
    share(1)
    own[4].wait()
    hid_copy = send(hid, hid_out, hid_sem.at[0], hid_sem.at[1], (other, c, m))
    own[3].wait()

    def red_copy(i, d):
        t = lax.rem(m + d, n)
        return pltpu.make_async_remote_copy(
            src_ref=part.at[i, t],
            dst_ref=red.at[i, d - 1],
            send_sem=red_send.at[i, d - 1],
            recv_sem=red_recv.at[i, d - 1],
            device_id=(s, c, t),
            device_id_type=MESH,
        )

    def project(i):
        arrive(i)
        r = block_of(c, i)

        @pl.loop(1, n + 1)
        def _(d):
            t = lax.rem(m + d, n)
            piece = w[pl.ds(pl.multiple_of(t * cut, cut), cut), :]
            part[i, t] = dot(piece, ctx[r], NT).astype(jnp.bfloat16)

            @pl.when(d < n)
            def _():
                red_copy(i, d).start()

    def z_copy(i, source, target):
        return pltpu.make_async_remote_copy(
            src_ref=zsrc.at[i],
            dst_ref=zin.at[source],
            send_sem=z_send.at[i],
            recv_sem=z_recv.at[source],
            device_id=(s, target, m),
            device_id_type=MESH,
        )

    def reduce(i):
        for d in range(1, n):
            red_copy(i, d).wait_recv()
        acc = part[i, m].astype(jnp.float32)
        for d in range(1, n):
            acc = acc + red[i, d - 1].astype(jnp.float32)
        if i == n - 1:
            zin[c] = acc.astype(jnp.bfloat16)
        else:
            zsrc[i] = acc.astype(jnp.bfloat16)
            z_copy(i, c, block_of(c, i)).start()

    out_copies = []

    def hand_over(source, own_plane=False):
        if not own_plane:
            z_copy(0, source, source).wait_recv()
        slot = len(out_copies)
        piece = branch_out.at[pl.ds(pl.multiple_of(m * cut, cut), cut)]
        out_copies.append(send(zin.at[source], piece, out_send.at[slot], out_recv.at[m], (other, c, source)))

    project(0)
    for i in range(2, n):
        share(i)
        project(i - 1)
        if i > 2:
            reduce(i - 3)
    project(n - 1)
    ctx_back = pltpu.make_async_copy(ctx.at[c], ctx_out, local_sem.at[5])
    ctx_back.start()
    reduce(1)
    reduce(2)
    hand_over(far)
    hand_over(far + 1)
    reduce(3)
    hand_over(c, own_plane=True)
    hand_over(mate)

    ctx_back.wait()
    for group in qkv_copies + [out_copies]:
        for copy in group:
            copy.wait_send()
    hid_copy.wait()
    for i in range(n):
        ctx_sent(i)
        if i < n - 1:
            z_copy(i, c, block_of(c, i)).wait_send()
        for d in range(1, n):
            red_copy(i, d).wait_send()
    for g in range(n):
        pltpu.make_async_remote_copy(
            src_ref=zin.at[0],
            dst_ref=branch_out.at[pl.ds(g * cut, cut)],
            send_sem=out_send.at[0],
            recv_sem=out_recv.at[g],
            device_id=(other, c, g),
            device_id_type=MESH,
        ).wait_recv()


def relay_body(n, hidden, query, keys, values, w_out):
    rows, inner = query.shape[1:]
    depth = hidden.shape[2]
    wide = inner // n
    heads = wide // HEAD_DIM
    cut = -(-depth // (16 * n)) * 16
    bf16 = jnp.bfloat16
    dma = pltpu.SemaphoreType.DMA
    hbm = pl.BlockSpec(memory_space=pltpu.HBM)
    branch, carried, context = pl.pallas_call(
        functools.partial(relay_kernel, n),
        out_shape=(
            jax.ShapeDtypeStruct((n * cut, rows), bf16),
            jax.ShapeDtypeStruct((depth, rows), bf16),
            jax.ShapeDtypeStruct((rows, inner), bf16),
        ),
        in_specs=[hbm] * 5,
        out_specs=(hbm,) * 3,
        scratch_shapes=[
            pltpu.VMEM((3, rows, inner), bf16),
            pltpu.VMEM((depth, rows), bf16),
            pltpu.VMEM((3, n, rows, wide), bf16),
            pltpu.VMEM((n * cut, inner), bf16),
            pltpu.VMEM((n, heads * rows, n * rows), bf16),
            pltpu.VMEM((n, rows, wide), jnp.float32),
            pltpu.VMEM((n, rows, inner), bf16),
            pltpu.VMEM((n, n, cut, rows), bf16),
            pltpu.VMEM((n, n - 1, cut, rows), bf16),
            pltpu.VMEM((n, cut, rows), bf16),
            pltpu.VMEM((n, cut, rows), bf16),
            dma((6,)),
            dma((3, n - 1)),
            dma((3, n - 1)),
            dma((2,)),
            dma((3, n)),
            dma((4, n)),
            dma((n, n - 1)),
            dma((n, n - 1)),
            dma((n,)),
            dma((n,)),
            dma((n,)),
            dma((n,)),
        ],
        compiler_params=pltpu.CompilerParams(
            collective_id=0, has_side_effects=True, vmem_limit_bytes=60 * 2**20
        ),
    )(query[0], keys[0], values[0], w_out[0], hidden[0].T)
    handed, context = pl.pallas_call(
        finish_kernel,
        out_shape=(
            jax.ShapeDtypeStruct((depth, rows), bf16),
            jax.ShapeDtypeStruct((rows, inner), bf16),
        ),
        in_specs=[hbm] * 3,
        out_specs=(hbm,) * 2,
        scratch_shapes=[pltpu.VMEM((depth, rows), bf16)] * 3 + [pltpu.VMEM((rows, inner), bf16), dma((5,))],
        compiler_params=pltpu.CompilerParams(vmem_limit_bytes=60 * 2**20),
    )(carried, branch, context)
    return (handed.T[None], context[None])


def finish_kernel(carried, branch, context, handed, context_out, first, second, summed, kept, sem):
    depth = handed.shape[0]
    one = pltpu.make_async_copy(carried, first, sem.at[0])
    two = pltpu.make_async_copy(branch.at[pl.ds(0, depth)], second, sem.at[1])
    three = pltpu.make_async_copy(context, kept, sem.at[2])
    for copy in (one, two, three):
        copy.start()
    three.wait()
    last = pltpu.make_async_copy(kept, context_out, sem.at[3])
    last.start()
    one.wait()
    two.wait()
    summed[...] = (first[...].astype(jnp.float32) + second[...].astype(jnp.float32)).astype(jnp.bfloat16)
    result = pltpu.make_async_copy(summed, handed, sem.at[4])
    result.start()
    last.wait()
    result.wait()


def from_behind(block, axis, distance):
    devices = range(lax.axis_size(axis))
    route = [((i - distance) % len(devices), i) for i in devices]
    return lax.ppermute(block, axis, route)


def head_scores(query_h, keys_h):
    return jnp.einsum("qd,kd->qk", query_h, keys_h, preferred_element_type=jnp.float32)


def body(hidden, query, keys, values, w_out):
    n = lax.axis_size("ctx")
    square = lax.axis_size("mp") == n and lax.axis_size("section") == 2
    if square and n == 4 and query.shape[2] % (128 * n) == 0 and query.shape[1] % 128 == 0:
        return relay_body(n, hidden, query, keys, values, w_out)
    rows = hidden[0]
    query_rows = query[0]
    inner_dev = query_rows.shape[1]
    heads_dev = inner_dev // HEAD_DIM
    keys_local = keys[0]
    values_local = values[0]
    keys_all, values_all = (
        lax.all_gather(keys_local, "ctx", axis=0, tiled=True),
        lax.all_gather(values_local, "ctx", axis=0, tiled=True),
    )
    pieces = []
    for head in range(heads_dev):
        lower = head * HEAD_DIM
        upper = lower + HEAD_DIM
        scores = head_scores(query_rows[:, lower:upper], keys_all[:, lower:upper])
        peak = jnp.max(scores, axis=1, keepdims=True)
        expo = jnp.exp(scores - peak)
        total = jnp.sum(expo, axis=1, keepdims=True)
        summed = jnp.dot(
            expo.astype(jnp.bfloat16),
            values_all[:, lower:upper],
            preferred_element_type=jnp.float32,
        )
        pieces.append(summed / total)
    context = jnp.concatenate(pieces, axis=1).astype(jnp.bfloat16)
    out_local = w_out[0]
    context_all = lax.all_gather(context, "ctx", axis=0, tiled=True)
    projected = jnp.einsum(
        "ri,di->rd", context_all, out_local, preferred_element_type=jnp.float32
    ).astype(jnp.bfloat16)
    branch_terms = lax.all_to_all(projected, "ctx", split_axis=0, concat_axis=1, tiled=True).astype(
        jnp.float32
    )
    branch = lax.psum_scatter(
        branch_terms.astype(jnp.bfloat16), "mp", scatter_dimension=1, tiled=True
    ).astype(jnp.float32)
    result = (rows.astype(jnp.float32) + branch).astype(jnp.bfloat16)
    handed = from_behind(result, "section", 1)
    return (handed[None], context[None])


def solution(mesh):
    in_specs = (
        P("section", "ctx", "mp"),
        P("section", "ctx", "mp"),
        P("section", "ctx", "mp"),
        P("section", "ctx", "mp"),
        P("section", "ctx", "mp"),
    )
    out_specs = (P("section", "ctx", "mp"), P("section", "ctx", "mp"))
    return jax.shard_map(body, mesh=mesh, in_specs=in_specs, out_specs=out_specs, check_vma=False)
```

```python
import functools

import jax
import jax.numpy as jnp
from jax import lax
from jax.experimental import pallas as pl
from jax.experimental.pallas import tpu as pltpu
from jax.sharding import PartitionSpec as P

HEAD_DIM = 64
MESH = pl.DeviceIdType.MESH
NT = (((1,), (1,)), ((), ()))


def dot(a, b, dims=(((1,), (0,)), ((), ()))):
    return lax.dot_general(a, b, dims, preferred_element_type=jnp.float32)


def relay_kernel(
    n,
    q_hbm,
    k_hbm,
    v_hbm,
    w_hbm,
    hid_hbm,
    branch_out,
    hid_out,
    ctx_out,
    staged,
    hid,
    qkv,
    w,
    w_pair,
    expo,
    total,
    ctx,
    ctx_pair,
    part,
    red,
    zsrc,
    zin,
    local_sem,
    qkv_send,
    qkv_recv,
    hid_sem,
    ctx_send,
    ctx_recv,
    pair_send,
    pair_recv,
    red_send,
    red_recv,
    z_send,
    z_recv,
    out_send,
    out_recv,
):
    s = lax.axis_index("section")
    c = lax.axis_index("ctx")
    m = lax.axis_index("mp")
    other = 1 - s
    x_mate = m + 1 - 2 * lax.rem(m, 2)
    y_mate = lax.rem(m + 2, n)
    pair_mate = jnp.where(s == 0, x_mate, y_mate)
    sum_mate = jnp.where(s == 0, y_mate, x_mate)
    wide = ctx.shape[2] // n
    rows = ctx.shape[1]
    depth = w_hbm.shape[0]
    cut = zsrc.shape[1]

    def columns(j):
        return pl.ds(pl.multiple_of(j * wide, wide), wide)

    def send(src, dst, send_sem, recv_sem, device):
        copy = pltpu.make_async_remote_copy(
            src_ref=src,
            dst_ref=dst,
            send_sem=send_sem,
            recv_sem=recv_sem,
            device_id=device,
            device_id_type=MESH,
        )
        copy.start()
        return copy

    inputs = (k_hbm, q_hbm, v_hbm)
    own = [pltpu.make_async_copy(ref, staged.at[i], local_sem.at[i]) for i, ref in enumerate(inputs)]
    own.append(pltpu.make_async_copy(w_hbm, w.at[pl.ds(0, depth)], local_sem.at[3]))
    own.append(pltpu.make_async_copy(hid_hbm, hid, local_sem.at[4]))
    for copy in own:
        copy.start()

    if n * cut > depth:
        w[depth:] = jnp.zeros((n * cut - depth, w.shape[1]), w.dtype)

    barrier = pltpu.get_barrier_semaphore()
    for d in range(1, n):
        pl.semaphore_signal(barrier, inc=1, device_id=(s, lax.rem(c + d, n), m), device_id_type=MESH)
        pl.semaphore_signal(barrier, inc=1, device_id=(s, c, lax.rem(m + d, n)), device_id_type=MESH)
    for a in range(n):
        pl.semaphore_signal(barrier, inc=1, device_id=(other, c, a), device_id_type=MESH)
    pl.semaphore_wait(barrier, 3 * n - 2)

    qkv_copies = []
    for i in range(3):
        own[i].wait()
        group = []
        for d in range(1, n):
            j = lax.rem(c + d, n)
            group.append(
                send(staged.at[i, :, columns(j)], qkv.at[i, c], qkv_send.at[i, d - 1], qkv_recv.at[i, d - 1], (s, j, m))
            )
        qkv_copies.append(group)
    own[3].wait()
    w_copies = []
    for i, t in enumerate((pair_mate, n - 1 - m)):
        piece = w.at[pl.ds(pl.multiple_of(t * cut, cut), cut)]
        w_copies.append(send(piece, w_pair.at[i], pair_send.at[3, i], pair_recv.at[3, i], (s, c, pair_mate)))
    for i in range(3):
        qkv[i, c] = staged[i, :, columns(c)]

    lane = lax.broadcasted_iota(jnp.int32, (rows, wide), 1) // HEAD_DIM
    heads = wide // HEAD_DIM
    masks = [jnp.where(lane == h, 1.0, 0.0).astype(jnp.bfloat16) for h in range(heads)]
    for i in (0, 1):
        for copy in qkv_copies[i]:
            copy.wait_recv()

    @pl.loop(0, n)
    def _(r):
        keys_all = qkv[0].reshape(n * rows, wide)
        q_r = qkv[1, r]
        scores = dot(jnp.concatenate([q_r * mask for mask in masks], axis=0), keys_all, NT)
        e = jnp.exp(scores - jnp.max(scores, axis=1, keepdims=True))
        sums = jnp.sum(e, axis=1, keepdims=True)
        wide_sum = jnp.broadcast_to(sums[:rows], (rows, wide))
        for h in range(1, heads):
            wide_sum = jnp.where(lane == h, sums[h * rows : (h + 1) * rows], wide_sum)
        total[r] = wide_sum
        expo[r] = e.astype(jnp.bfloat16)

    for copy in qkv_copies[2]:
        copy.wait_recv()

    @pl.loop(0, n)
    def _(r):
        values_all = qkv[2].reshape(n * rows, wide)
        both = dot(expo[r], values_all)
        picked = both[:rows]
        for h in range(1, heads):
            picked = jnp.where(lane == h, both[h * rows : (h + 1) * rows], picked)
        ctx[r, :, columns(c)] = (picked / total[r]).astype(jnp.bfloat16)

    inner = (c == 1) | (c == 2)
    mate = c + 1 - 2 * lax.rem(c, 2)
    far = jnp.where(c < 2, 2, 0)
    far_inner = jnp.where(c < 2, 2, 1)

    def pair_block(plane, i):
        return jnp.where(plane < 2, n - 1 - i, i)

    def block_of(plane, i):
        if i < 2:
            return pair_block(plane, i)
        return pair_block(plane, jnp.where((plane == 1) | (plane == 2), 5 - i, i))

    def ctx_copy(block, kind, i, arrival, target):
        return pltpu.make_async_remote_copy(
            src_ref=block,
            dst_ref=block,
            send_sem=ctx_send.at[kind, i],
            recv_sem=ctx_recv.at[arrival, i],
            device_id=(s, target, m),
            device_id_type=MESH,
        )

    def when(condition, action):
        @pl.when(condition)
        def _():
            action()

    def to_mate(i):
        return ctx_copy(ctx.at[block_of(mate, i), :, columns(c)], 0, i, 0, mate)

    def to_far(i):
        block = ctx.at[pair_block(far_inner, i), :, columns(c)]
        return ctx_copy(block, 1, i, 1 + lax.rem(c, 2), far_inner)

    def relayed(i):
        both = pl.ds(pl.multiple_of(far * wide, wide), 2 * wide)
        return ctx_copy(ctx.at[pair_block(c, i), :, both], 2, i, 3, mate)

    def pass_on(kind, i):
        first = (c, mate, far)[kind]
        width = wide * (1, 1, 2)[kind]
        span = pl.ds(pl.multiple_of(first * wide, wide), width)
        r = block_of(c, i)
        return pltpu.make_async_remote_copy(
            src_ref=ctx.at[r, :, span],
            dst_ref=ctx_pair.at[r, :, span],
            send_sem=pair_send.at[kind, i],
            recv_sem=pair_recv.at[kind, i],
            device_id=(s, c, pair_mate),
            device_id_type=MESH,
        )

    def share(i):
        to_far(i).start()
        to_mate(i).start()
        pass_on(0, i).start()

    def relay(i):
        for k in range(2):
            block = ctx.at[pair_block(c, i), :, columns(far + k)]
            ctx_copy(block, 1, i, 1 + k, far_inner).wait_recv()
        relayed(i).start()

    def arrive(i):
        for k in ((i,), (i,), (2, 3), ())[i]:
            when(inner, lambda: relay(k))
        when(~inner, lambda: relayed(i).wait_recv())
        pass_on(2, i).start()
        ctx_copy(ctx.at[block_of(c, i), :, columns(mate)], 0, i, 0, mate).wait_recv()
        pass_on(1, i).start()

    def ctx_sent(i):
        to_far(i).wait_send()
        to_mate(i).wait_send()
        when(inner, lambda: relayed(i).wait_send())

    share(0)
    share(1)
    own[4].wait()
    hid_copy = send(hid, hid_out, hid_sem.at[0], hid_sem.at[1], (other, c, m))

    def red_copy(i):
        return pltpu.make_async_remote_copy(
            src_ref=part.at[i, 1],
            dst_ref=red.at[i],
            send_sem=red_send.at[i],
            recv_sem=red_recv.at[i],
            device_id=(s, c, sum_mate),
            device_id_type=MESH,
        )

    def project(i):
        for kind in range(3):
            pass_on(kind, i).wait_recv()
        if i == 0:
            for copy in w_copies:
                copy.wait_recv()
        r = block_of(c, i)

        @pl.loop(0, 2)
        def _(k):
            t = jnp.where(k == 0, sum_mate, m)
            piece = w[pl.ds(pl.multiple_of(t * cut, cut), cut), :]
            both = dot(piece, ctx[r], NT) + dot(w_pair[1 - k], ctx_pair[r], NT)
            part[i, 1 - k] = both.astype(jnp.bfloat16)

            @pl.when(k == 0)
            def _():
                red_copy(i).start()

    def z_copy(i, source, target):
        return pltpu.make_async_remote_copy(
            src_ref=zsrc.at[i],
            dst_ref=zin.at[source],
            send_sem=z_send.at[i],
            recv_sem=z_recv.at[source],
            device_id=(s, target, m),
            device_id_type=MESH,
        )

    def reduce(i):
        red_copy(i).wait_recv()
        acc = part[i, 0].astype(jnp.float32) + red[i].astype(jnp.float32)
        if i == n - 1:
            zin[c] = acc.astype(jnp.bfloat16)
        else:
            zsrc[i] = acc.astype(jnp.bfloat16)
            z_copy(i, c, block_of(c, i)).start()

    out_copies = []

    def hand_over(source, own_plane=False):
        if not own_plane:
            z_copy(0, source, source).wait_recv()
        slot = len(out_copies)
        piece = branch_out.at[pl.ds(pl.multiple_of(m * cut, cut), cut)]
        out_copies.append(send(zin.at[source], piece, out_send.at[slot], out_recv.at[m], (other, c, source)))

    arrive(0)
    for i in range(n - 1):
        if i + 2 < n:
            share(i + 2)
        arrive(i + 1)
        project(i)
        if i > 0:
            reduce(i - 1)
    ctx_back = pltpu.make_async_copy(ctx.at[c], ctx_out, local_sem.at[5])
    ctx_back.start()
    project(n - 1)
    reduce(2)
    hand_over(far)
    hand_over(far + 1)
    reduce(3)
    hand_over(c, own_plane=True)
    hand_over(mate)

    ctx_back.wait()
    for group in qkv_copies + [w_copies, out_copies]:
        for copy in group:
            copy.wait_send()
    hid_copy.wait()
    for i in range(n):
        ctx_sent(i)
        if i < n - 1:
            z_copy(i, c, block_of(c, i)).wait_send()
        red_copy(i).wait_send()
        for kind in range(3):
            pass_on(kind, i).wait_send()
    for g in range(n):
        pltpu.make_async_remote_copy(
            src_ref=zin.at[0],
            dst_ref=branch_out.at[pl.ds(g * cut, cut)],
            send_sem=out_send.at[0],
            recv_sem=out_recv.at[g],
            device_id=(other, c, g),
            device_id_type=MESH,
        ).wait_recv()


def relay_body(n, hidden, query, keys, values, w_out):
    rows, inner = query.shape[1:]
    depth = hidden.shape[2]
    wide = inner // n
    heads = wide // HEAD_DIM
    cut = -(-depth // (16 * n)) * 16
    bf16 = jnp.bfloat16
    dma = pltpu.SemaphoreType.DMA
    hbm = pl.BlockSpec(memory_space=pltpu.HBM)
    branch, carried, context = pl.pallas_call(
        functools.partial(relay_kernel, n),
        out_shape=(
            jax.ShapeDtypeStruct((n * cut, rows), bf16),
            jax.ShapeDtypeStruct((depth, rows), bf16),
            jax.ShapeDtypeStruct((rows, inner), bf16),
        ),
        in_specs=[hbm] * 5,
        out_specs=(hbm,) * 3,
        scratch_shapes=[
            pltpu.VMEM((3, rows, inner), bf16),
            pltpu.VMEM((depth, rows), bf16),
            pltpu.VMEM((3, n, rows, wide), bf16),
            pltpu.VMEM((n * cut, inner), bf16),
            pltpu.VMEM((2, cut, inner), bf16),
            pltpu.VMEM((n, heads * rows, n * rows), bf16),
            pltpu.VMEM((n, rows, wide), jnp.float32),
            pltpu.VMEM((n, rows, inner), bf16),
            pltpu.VMEM((n, rows, inner), bf16),
            pltpu.VMEM((n, 2, cut, rows), bf16),
            pltpu.VMEM((n, cut, rows), bf16),
            pltpu.VMEM((n, cut, rows), bf16),
            pltpu.VMEM((n, cut, rows), bf16),
            dma((6,)),
            dma((3, n - 1)),
            dma((3, n - 1)),
            dma((2,)),
            dma((3, n)),
            dma((4, n)),
            dma((4, n)),
            dma((4, n)),
            dma((n,)),
            dma((n,)),
            dma((n,)),
            dma((n,)),
            dma((n,)),
            dma((n,)),
        ],
        compiler_params=pltpu.CompilerParams(
            collective_id=0, has_side_effects=True, vmem_limit_bytes=60 * 2**20
        ),
    )(query[0], keys[0], values[0], w_out[0], hidden[0].T)
    handed, context = pl.pallas_call(
        finish_kernel,
        out_shape=(
            jax.ShapeDtypeStruct((depth, rows), bf16),
            jax.ShapeDtypeStruct((rows, inner), bf16),
        ),
        in_specs=[hbm] * 3,
        out_specs=(hbm,) * 2,
        scratch_shapes=[pltpu.VMEM((depth, rows), bf16)] * 3 + [pltpu.VMEM((rows, inner), bf16), dma((5,))],
        compiler_params=pltpu.CompilerParams(vmem_limit_bytes=60 * 2**20),
    )(carried, branch, context)
    return (handed.T[None], context[None])


def finish_kernel(carried, branch, context, handed, context_out, first, second, summed, kept, sem):
    depth = handed.shape[0]
    one = pltpu.make_async_copy(carried, first, sem.at[0])
    two = pltpu.make_async_copy(branch.at[pl.ds(0, depth)], second, sem.at[1])
    three = pltpu.make_async_copy(context, kept, sem.at[2])
    for copy in (one, two, three):
        copy.start()
    three.wait()
    last = pltpu.make_async_copy(kept, context_out, sem.at[3])
    last.start()
    one.wait()
    two.wait()
    summed[...] = (first[...].astype(jnp.float32) + second[...].astype(jnp.float32)).astype(jnp.bfloat16)
    result = pltpu.make_async_copy(summed, handed, sem.at[4])
    result.start()
    last.wait()
    result.wait()


def from_behind(block, axis, distance):
    devices = range(lax.axis_size(axis))
    route = [((i - distance) % len(devices), i) for i in devices]
    return lax.ppermute(block, axis, route)


def head_scores(query_h, keys_h):
    return jnp.einsum("qd,kd->qk", query_h, keys_h, preferred_element_type=jnp.float32)


def body(hidden, query, keys, values, w_out):
    n = lax.axis_size("ctx")
    square = lax.axis_size("mp") == n and lax.axis_size("section") == 2
    if square and n == 4 and query.shape[2] % (128 * n) == 0 and query.shape[1] % 128 == 0:
        return relay_body(n, hidden, query, keys, values, w_out)
    rows = hidden[0]
    query_rows = query[0]
    inner_dev = query_rows.shape[1]
    heads_dev = inner_dev // HEAD_DIM
    keys_local = keys[0]
    values_local = values[0]
    keys_all, values_all = (
        lax.all_gather(keys_local, "ctx", axis=0, tiled=True),
        lax.all_gather(values_local, "ctx", axis=0, tiled=True),
    )
    pieces = []
    for head in range(heads_dev):
        lower = head * HEAD_DIM
        upper = lower + HEAD_DIM
        scores = head_scores(query_rows[:, lower:upper], keys_all[:, lower:upper])
        peak = jnp.max(scores, axis=1, keepdims=True)
        expo = jnp.exp(scores - peak)
        total = jnp.sum(expo, axis=1, keepdims=True)
        summed = jnp.dot(
            expo.astype(jnp.bfloat16),
            values_all[:, lower:upper],
            preferred_element_type=jnp.float32,
        )
        pieces.append(summed / total)
    context = jnp.concatenate(pieces, axis=1).astype(jnp.bfloat16)
    out_local = w_out[0]
    context_all = lax.all_gather(context, "ctx", axis=0, tiled=True)
    projected = jnp.einsum(
        "ri,di->rd", context_all, out_local, preferred_element_type=jnp.float32
    ).astype(jnp.bfloat16)
    branch_terms = lax.all_to_all(projected, "ctx", split_axis=0, concat_axis=1, tiled=True).astype(
        jnp.float32
    )
    branch = lax.psum_scatter(
        branch_terms.astype(jnp.bfloat16), "mp", scatter_dimension=1, tiled=True
    ).astype(jnp.float32)
    result = (rows.astype(jnp.float32) + branch).astype(jnp.bfloat16)
    handed = from_behind(result, "section", 1)
    return (handed[None], context[None])


def solution(mesh):
    in_specs = (
        P("section", "ctx", "mp"),
        P("section", "ctx", "mp"),
        P("section", "ctx", "mp"),
        P("section", "ctx", "mp"),
        P("section", "ctx", "mp"),
    )
    out_specs = (P("section", "ctx", "mp"), P("section", "ctx", "mp"))
    return jax.shard_map(body, mesh=mesh, in_specs=in_specs, out_specs=out_specs, check_vma=False)
```

```python
import functools

import jax
import jax.numpy as jnp
from jax import lax
from jax.experimental import pallas as pl
from jax.experimental.pallas import tpu as pltpu
from jax.sharding import PartitionSpec as P

HEAD_DIM = 64
MESH = pl.DeviceIdType.MESH
NT = (((1,), (1,)), ((), ()))


def dot(a, b, dims=(((1,), (0,)), ((), ()))):
    return lax.dot_general(a, b, dims, preferred_element_type=jnp.float32)


def relay_kernel(
    n,
    shifts,
    q_hbm,
    k_hbm,
    v_hbm,
    w_hbm,
    hid_hbm,
    branch_out,
    hid_out,
    ctx_out,
    staged,
    hid,
    qkv,
    w,
    expo,
    total,
    ctx,
    part,
    red,
    zsrc,
    zin,
    local_sem,
    qkv_send,
    qkv_recv,
    hid_sem,
    ctx_send,
    ctx_recv,
    red_send,
    red_recv,
    z_send,
    z_recv,
    out_send,
    out_recv,
):
    s = lax.axis_index("section")
    c = lax.axis_index("ctx")
    m = lax.axis_index("mp")
    other = 1 - s
    x_mate = m + 1 - 2 * lax.rem(m, 2)
    y_mate = lax.rem(m + 2, n)
    first_mate = jnp.where(s == 0, x_mate, y_mate)
    second_mate = jnp.where(s == 0, y_mate, x_mate)

    def mate(d):
        return jnp.where(d == 1, first_mate, jnp.where(d == 2, second_mate, jnp.where(d == 3, n - 1 - m, m)))

    wide = ctx.shape[2] // n
    rows = ctx.shape[1]
    depth = w_hbm.shape[0]
    cut = zsrc.shape[1]

    def columns(j):
        return pl.ds(pl.multiple_of(j * wide, wide), wide)

    def send(src, dst, send_sem, recv_sem, device):
        copy = pltpu.make_async_remote_copy(
            src_ref=src,
            dst_ref=dst,
            send_sem=send_sem,
            recv_sem=recv_sem,
            device_id=device,
            device_id_type=MESH,
        )
        copy.start()
        return copy

    inputs = (k_hbm, q_hbm, v_hbm)
    own = [pltpu.make_async_copy(ref, staged.at[i], local_sem.at[i]) for i, ref in enumerate(inputs)]
    own.append(pltpu.make_async_copy(w_hbm, w.at[pl.ds(0, depth)], local_sem.at[3]))
    own.append(pltpu.make_async_copy(hid_hbm, hid, local_sem.at[4]))
    for copy in own:
        copy.start()

    if n * cut > depth:
        w[depth:] = jnp.zeros((n * cut - depth, w.shape[1]), w.dtype)

    barrier = pltpu.get_barrier_semaphore()
    for d in range(1, n):
        pl.semaphore_signal(barrier, inc=1, device_id=(s, lax.rem(c + d, n), m), device_id_type=MESH)
        pl.semaphore_signal(barrier, inc=1, device_id=(s, c, lax.rem(m + d, n)), device_id_type=MESH)
    for a in range(n):
        pl.semaphore_signal(barrier, inc=1, device_id=(other, c, a), device_id_type=MESH)
    pl.semaphore_wait(barrier, 3 * n - 2)

    qkv_copies = []
    for i in range(3):
        own[i].wait()
        group = []
        for d in range(1, n):
            j = lax.rem(c + d, n)
            group.append(
                send(staged.at[i, :, columns(j)], qkv.at[i, c], qkv_send.at[i, d - 1], qkv_recv.at[i, d - 1], (s, j, m))
            )
        qkv_copies.append(group)
    own[4].wait()
    hid_copy = send(hid, hid_out, hid_sem.at[0], hid_sem.at[1], (other, c, m))
    for i in range(3):
        qkv[i, c] = staged[i, :, columns(c)]

    lane = lax.broadcasted_iota(jnp.int32, (rows, wide), 1) // HEAD_DIM
    heads = wide // HEAD_DIM
    masks = [jnp.where(lane == h, 1.0, 0.0).astype(jnp.bfloat16) for h in range(heads)]
    for i in (0, 1):
        for copy in qkv_copies[i]:
            copy.wait_recv()

    @pl.loop(0, n)
    def _(r):
        keys_all = qkv[0].reshape(n * rows, wide)
        q_r = qkv[1, r]
        scores = dot(jnp.concatenate([q_r * mask for mask in masks], axis=0), keys_all, NT)
        e = jnp.exp(scores - jnp.max(scores, axis=1, keepdims=True))
        sums = jnp.sum(e, axis=1, keepdims=True)
        wide_sum = jnp.broadcast_to(sums[:rows], (rows, wide))
        for h in range(1, heads):
            wide_sum = jnp.where(lane == h, sums[h * rows : (h + 1) * rows], wide_sum)
        total[r] = wide_sum
        expo[r] = e.astype(jnp.bfloat16)

    for copy in qkv_copies[2]:
        copy.wait_recv()

    @pl.loop(0, n)
    def _(r):
        values_all = qkv[2].reshape(n * rows, wide)
        both = dot(expo[r], values_all)
        picked = both[:rows]
        for h in range(1, heads):
            picked = jnp.where(lane == h, both[h * rows : (h + 1) * rows], picked)
        ctx[r, :, columns(c)] = (picked / total[r]).astype(jnp.bfloat16)

    def share(i):
        group = []
        for d in range(1, n):
            j = lax.rem(c + d, n)
            block = ctx.at[lax.rem(j + shifts[i], n), :, columns(c)]
            group.append(send(block, block, ctx_send.at[i, d - 1], ctx_recv.at[i, d - 1], (s, j, m)))
        ctx_copies.append(group)

    ctx_copies = []
    share(0)
    share(1)
    own[3].wait()

    def red_copy(i, d):
        t = mate(d)
        return pltpu.make_async_remote_copy(
            src_ref=part.at[i, t],
            dst_ref=red.at[i, d - 1],
            send_sem=red_send.at[i, d - 1],
            recv_sem=red_recv.at[i, d - 1],
            device_id=(s, c, t),
            device_id_type=MESH,
        )

    def project(i):
        for d in range(1, n):
            block = ctx.at[lax.rem(c + shifts[i], n), :, columns(lax.rem(c + d, n))]
            pltpu.make_async_remote_copy(
                src_ref=block,
                dst_ref=block,
                send_sem=ctx_send.at[i, d - 1],
                recv_sem=ctx_recv.at[i, n - 1 - d],
                device_id=(s, lax.rem(c + d, n), m),
                device_id_type=MESH,
            ).wait_recv()
        r = lax.rem(c + shifts[i], n)

        @pl.loop(1, n + 1)
        def _(d):
            t = mate(d)
            piece = w[pl.ds(pl.multiple_of(t * cut, cut), cut), :]
            part[i, t] = dot(piece, ctx[r], NT).astype(jnp.bfloat16)

            @pl.when(d < n)
            def _():
                red_copy(i, d).start()

    z_copies = []

    def reduce(i):
        for d in range(1, n):
            red_copy(i, d).wait_recv()
        acc = part[i, m].astype(jnp.float32)
        for d in range(1, n):
            acc = acc + red[i, d - 1].astype(jnp.float32)
        if shifts[i] == 0:
            zin[i] = acc.astype(jnp.bfloat16)
        else:
            zsrc[i] = acc.astype(jnp.bfloat16)
            target = lax.rem(c + shifts[i], n)
            z_copies.append(send(zsrc.at[i], zin.at[i], z_send.at[i], z_recv.at[i], (s, target, m)))

    out_copies = []

    def hand_over(i):
        if shifts[i]:
            z_copies[i].wait_recv()
        target = lax.rem(c + n - shifts[i], n)
        piece = branch_out.at[pl.ds(pl.multiple_of(m * cut, cut), cut)]
        out_copies.append(send(zin.at[i], piece, out_send.at[i], out_recv.at[m], (other, c, target)))

    project(0)
    for i in range(2, n):
        share(i)
        project(i - 1)
        if i > 2:
            reduce(i - 3)
    project(n - 1)
    ctx_back = pltpu.make_async_copy(ctx.at[c], ctx_out, local_sem.at[5])
    ctx_back.start()
    for i in range(n - 3, n):
        reduce(i)
        if i < n - 1:
            hand_over(i - 1)
    hand_over(n - 1)
    hand_over(n - 2)

    ctx_back.wait()
    for group in qkv_copies + ctx_copies + [z_copies, out_copies]:
        for copy in group:
            copy.wait_send()
    hid_copy.wait()
    for i in range(n):
        for d in range(1, n):
            red_copy(i, d).wait_send()
    for g in range(n):
        pltpu.make_async_remote_copy(
            src_ref=zin.at[0],
            dst_ref=branch_out.at[pl.ds(g * cut, cut)],
            send_sem=out_send.at[0],
            recv_sem=out_recv.at[g],
            device_id=(other, c, g),
            device_id_type=MESH,
        ).wait_recv()


def relay_body(n, hidden, query, keys, values, w_out):
    rows, inner = query.shape[1:]
    depth = hidden.shape[2]
    wide = inner // n
    heads = wide // HEAD_DIM
    cut = -(-depth // (16 * n)) * 16
    bf16 = jnp.bfloat16
    dma = pltpu.SemaphoreType.DMA
    hbm = pl.BlockSpec(memory_space=pltpu.HBM)
    branch, carried, context = pl.pallas_call(
        functools.partial(relay_kernel, n, (2, 1, 3, 0)),
        out_shape=(
            jax.ShapeDtypeStruct((n * cut, rows), bf16),
            jax.ShapeDtypeStruct((depth, rows), bf16),
            jax.ShapeDtypeStruct((rows, inner), bf16),
        ),
        in_specs=[hbm] * 5,
        out_specs=(hbm,) * 3,
        scratch_shapes=[
            pltpu.VMEM((3, rows, inner), bf16),
            pltpu.VMEM((depth, rows), bf16),
            pltpu.VMEM((3, n, rows, wide), bf16),
            pltpu.VMEM((n * cut, inner), bf16),
            pltpu.VMEM((n, heads * rows, n * rows), bf16),
            pltpu.VMEM((n, rows, wide), jnp.float32),
            pltpu.VMEM((n, rows, inner), bf16),
            pltpu.VMEM((n, n, cut, rows), bf16),
            pltpu.VMEM((n, n - 1, cut, rows), bf16),
            pltpu.VMEM((n, cut, rows), bf16),
            pltpu.VMEM((n, cut, rows), bf16),
            dma((6,)),
            dma((3, n - 1)),
            dma((3, n - 1)),
            dma((2,)),
            dma((n, n - 1)),
            dma((n, n - 1)),
            dma((n, n - 1)),
            dma((n, n - 1)),
            dma((n,)),
            dma((n,)),
            dma((n,)),
            dma((n,)),
        ],
        compiler_params=pltpu.CompilerParams(
            collective_id=0, has_side_effects=True, vmem_limit_bytes=60 * 2**20
        ),
    )(query[0], keys[0], values[0], w_out[0], hidden[0].T)
    handed, context = pl.pallas_call(
        finish_kernel,
        out_shape=(
            jax.ShapeDtypeStruct((depth, rows), bf16),
            jax.ShapeDtypeStruct((rows, inner), bf16),
        ),
        in_specs=[hbm] * 3,
        out_specs=(hbm,) * 2,
        scratch_shapes=[pltpu.VMEM((depth, rows), bf16)] * 3 + [pltpu.VMEM((rows, inner), bf16), dma((5,))],
        compiler_params=pltpu.CompilerParams(vmem_limit_bytes=60 * 2**20),
    )(carried, branch, context)
    return (handed.T[None], context[None])


def finish_kernel(carried, branch, context, handed, context_out, first, second, summed, kept, sem):
    depth = handed.shape[0]
    one = pltpu.make_async_copy(carried, first, sem.at[0])
    two = pltpu.make_async_copy(branch.at[pl.ds(0, depth)], second, sem.at[1])
    three = pltpu.make_async_copy(context, kept, sem.at[2])
    for copy in (one, two, three):
        copy.start()
    three.wait()
    last = pltpu.make_async_copy(kept, context_out, sem.at[3])
    last.start()
    one.wait()
    two.wait()
    summed[...] = (first[...].astype(jnp.float32) + second[...].astype(jnp.float32)).astype(jnp.bfloat16)
    result = pltpu.make_async_copy(summed, handed, sem.at[4])
    result.start()
    last.wait()
    result.wait()


def from_behind(block, axis, distance):
    devices = range(lax.axis_size(axis))
    route = [((i - distance) % len(devices), i) for i in devices]
    return lax.ppermute(block, axis, route)


def head_scores(query_h, keys_h):
    return jnp.einsum("qd,kd->qk", query_h, keys_h, preferred_element_type=jnp.float32)


def body(hidden, query, keys, values, w_out):
    n = lax.axis_size("ctx")
    square = lax.axis_size("mp") == n and lax.axis_size("section") == 2
    if square and n == 4 and query.shape[2] % (128 * n) == 0 and query.shape[1] % 128 == 0:
        return relay_body(n, hidden, query, keys, values, w_out)
    rows = hidden[0]
    query_rows = query[0]
    inner_dev = query_rows.shape[1]
    heads_dev = inner_dev // HEAD_DIM
    keys_local = keys[0]
    values_local = values[0]
    keys_all, values_all = (
        lax.all_gather(keys_local, "ctx", axis=0, tiled=True),
        lax.all_gather(values_local, "ctx", axis=0, tiled=True),
    )
    pieces = []
    for head in range(heads_dev):
        lower = head * HEAD_DIM
        upper = lower + HEAD_DIM
        scores = head_scores(query_rows[:, lower:upper], keys_all[:, lower:upper])
        peak = jnp.max(scores, axis=1, keepdims=True)
        expo = jnp.exp(scores - peak)
        total = jnp.sum(expo, axis=1, keepdims=True)
        summed = jnp.dot(
            expo.astype(jnp.bfloat16),
            values_all[:, lower:upper],
            preferred_element_type=jnp.float32,
        )
        pieces.append(summed / total)
    context = jnp.concatenate(pieces, axis=1).astype(jnp.bfloat16)
    out_local = w_out[0]
    context_all = lax.all_gather(context, "ctx", axis=0, tiled=True)
    projected = jnp.einsum(
        "ri,di->rd", context_all, out_local, preferred_element_type=jnp.float32
    ).astype(jnp.bfloat16)
    branch_terms = lax.all_to_all(projected, "ctx", split_axis=0, concat_axis=1, tiled=True).astype(
        jnp.float32
    )
    branch = lax.psum_scatter(
        branch_terms.astype(jnp.bfloat16), "mp", scatter_dimension=1, tiled=True
    ).astype(jnp.float32)
    result = (rows.astype(jnp.float32) + branch).astype(jnp.bfloat16)
    handed = from_behind(result, "section", 1)
    return (handed[None], context[None])


def solution(mesh):
    in_specs = (
        P("section", "ctx", "mp"),
        P("section", "ctx", "mp"),
        P("section", "ctx", "mp"),
        P("section", "ctx", "mp"),
        P("section", "ctx", "mp"),
    )
    out_specs = (P("section", "ctx", "mp"), P("section", "ctx", "mp"))
    return jax.shard_map(body, mesh=mesh, in_specs=in_specs, out_specs=out_specs, check_vma=False)
```

```python
import functools

import jax
import jax.numpy as jnp
from jax import lax
from jax.experimental import pallas as pl
from jax.experimental.pallas import tpu as pltpu
from jax.sharding import PartitionSpec as P

HEAD_DIM = 64
MESH = pl.DeviceIdType.MESH
NT = (((1,), (1,)), ((), ()))


def dot(a, b, dims=(((1,), (0,)), ((), ()))):
    return lax.dot_general(a, b, dims, preferred_element_type=jnp.float32)


def relay_kernel(
    n,
    shifts,
    q_hbm,
    k_hbm,
    v_hbm,
    w_hbm,
    hid_hbm,
    branch_out,
    hid_out,
    ctx_out,
    staged,
    hid,
    qkv,
    w,
    expo,
    total,
    ctx,
    part,
    red,
    zsrc,
    zin,
    local_sem,
    qkv_send,
    qkv_recv,
    hid_sem,
    ctx_send,
    ctx_recv,
    red_send,
    red_recv,
    z_send,
    z_recv,
    out_send,
    out_recv,
):
    s = lax.axis_index("section")
    c = lax.axis_index("ctx")
    m = lax.axis_index("mp")
    other = 1 - s
    x_mate = m + 1 - 2 * lax.rem(m, 2)
    y_mate = lax.rem(m + 2, n)
    first_mate = jnp.where(s == 0, x_mate, y_mate)
    second_mate = jnp.where(s == 0, y_mate, x_mate)

    def mate(d):
        return jnp.where(d == 1, first_mate, jnp.where(d == 2, second_mate, jnp.where(d == 3, n - 1 - m, m)))

    wide = ctx.shape[2] // n
    rows = ctx.shape[1]
    depth = w_hbm.shape[0]
    cut = zsrc.shape[1]

    def columns(j):
        return pl.ds(pl.multiple_of(j * wide, wide), wide)

    def send(src, dst, send_sem, recv_sem, device):
        copy = pltpu.make_async_remote_copy(
            src_ref=src,
            dst_ref=dst,
            send_sem=send_sem,
            recv_sem=recv_sem,
            device_id=device,
            device_id_type=MESH,
        )
        copy.start()
        return copy

    inputs = (k_hbm, q_hbm, v_hbm)
    own = [pltpu.make_async_copy(ref, staged.at[i], local_sem.at[i]) for i, ref in enumerate(inputs)]
    own.append(pltpu.make_async_copy(w_hbm, w.at[pl.ds(0, depth)], local_sem.at[3]))
    own.append(pltpu.make_async_copy(hid_hbm, hid, local_sem.at[4]))
    for copy in own:
        copy.start()

    if n * cut > depth:
        w[depth:] = jnp.zeros((n * cut - depth, w.shape[1]), w.dtype)

    barrier = pltpu.get_barrier_semaphore()
    for d in range(1, n):
        pl.semaphore_signal(barrier, inc=1, device_id=(s, lax.rem(c + d, n), m), device_id_type=MESH)
        pl.semaphore_signal(barrier, inc=1, device_id=(s, c, lax.rem(m + d, n)), device_id_type=MESH)
    for a in range(n):
        pl.semaphore_signal(barrier, inc=1, device_id=(other, c, a), device_id_type=MESH)
    pl.semaphore_wait(barrier, 3 * n - 2)

    qkv_copies = []
    for i in range(3):
        own[i].wait()
        group = []
        for d in range(1, n):
            j = lax.rem(c + d, n)
            group.append(
                send(staged.at[i, :, columns(j)], qkv.at[i, c], qkv_send.at[i, d - 1], qkv_recv.at[i, d - 1], (s, j, m))
            )
        qkv_copies.append(group)
    own[4].wait()
    hid_copy = send(hid, hid_out, hid_sem.at[0], hid_sem.at[1], (other, c, m))
    for i in range(3):
        qkv[i, c] = staged[i, :, columns(c)]

    lane = lax.broadcasted_iota(jnp.int32, (rows, wide), 1) // HEAD_DIM
    heads = wide // HEAD_DIM
    masks = [jnp.where(lane == h, 1.0, 0.0).astype(jnp.bfloat16) for h in range(heads)]
    for i in (0, 1):
        for copy in qkv_copies[i]:
            copy.wait_recv()

    @pl.loop(0, n)
    def _(r):
        keys_all = qkv[0].reshape(n * rows, wide)
        q_r = qkv[1, r]
        scores = dot(jnp.concatenate([q_r * mask for mask in masks], axis=0), keys_all, NT)
        e = jnp.exp(scores - jnp.max(scores, axis=1, keepdims=True))
        sums = jnp.sum(e, axis=1, keepdims=True)
        wide_sum = jnp.broadcast_to(sums[:rows], (rows, wide))
        for h in range(1, heads):
            wide_sum = jnp.where(lane == h, sums[h * rows : (h + 1) * rows], wide_sum)
        total[r] = wide_sum
        expo[r] = e.astype(jnp.bfloat16)

    for copy in qkv_copies[2]:
        copy.wait_recv()

    @pl.loop(0, n)
    def _(r):
        values_all = qkv[2].reshape(n * rows, wide)
        both = dot(expo[r], values_all)
        picked = both[:rows]
        for h in range(1, heads):
            picked = jnp.where(lane == h, both[h * rows : (h + 1) * rows], picked)
        ctx[r, :, columns(c)] = (picked / total[r]).astype(jnp.bfloat16)

    def share(i):
        group = []
        for d in range(1, n):
            j = lax.rem(c + d, n)
            block = ctx.at[lax.rem(j + shifts[i], n), :, columns(c)]
            group.append(send(block, block, ctx_send.at[i, d - 1], ctx_recv.at[i, d - 1], (s, j, m)))
        ctx_copies.append(group)

    ctx_copies = []
    share(0)
    share(1)
    own[3].wait()

    def red_copy(i, d):
        target = mate(d) if i == n - 1 else jnp.where(d == 3, first_mate, mate(d))
        return pltpu.make_async_remote_copy(
            src_ref=part.at[i, mate(d)],
            dst_ref=red.at[i, d - 1],
            send_sem=red_send.at[i, d - 1],
            recv_sem=red_recv.at[i, d - 1],
            device_id=(s, c, target),
            device_id_type=MESH,
        )

    def combine(i):
        red_copy(i, 3).wait_recv()
        both = part[i, second_mate].astype(jnp.float32) + red[i, 2].astype(jnp.float32)
        part[i, second_mate] = both.astype(jnp.bfloat16)
        red_copy(i, 2).start()

    def project(i):
        for d in range(1, n):
            block = ctx.at[lax.rem(c + shifts[i], n), :, columns(lax.rem(c + d, n))]
            pltpu.make_async_remote_copy(
                src_ref=block,
                dst_ref=block,
                send_sem=ctx_send.at[i, d - 1],
                recv_sem=ctx_recv.at[i, n - 1 - d],
                device_id=(s, lax.rem(c + d, n), m),
                device_id_type=MESH,
            ).wait_recv()
        r = lax.rem(c + shifts[i], n)

        @pl.loop(1, n + 1)
        def _(step):
            d = jnp.where(step == 2, 3, jnp.where(step == 3, 2, step))
            t = mate(d)
            piece = w[pl.ds(pl.multiple_of(t * cut, cut), cut), :]
            part[i, t] = dot(piece, ctx[r], NT).astype(jnp.bfloat16)

            @pl.when((d < n) if i == n - 1 else (step < 3))
            def _():
                red_copy(i, d).start()

    z_copies = []

    def reduce(i):
        acc = part[i, m].astype(jnp.float32)
        for d in (1, 2, 3) if i == n - 1 else (1, 2):
            red_copy(i, d).wait_recv()
            acc = acc + red[i, d - 1].astype(jnp.float32)
        if shifts[i] == 0:
            zin[i] = acc.astype(jnp.bfloat16)
        else:
            zsrc[i] = acc.astype(jnp.bfloat16)
            target = lax.rem(c + shifts[i], n)
            z_copies.append(send(zsrc.at[i], zin.at[i], z_send.at[i], z_recv.at[i], (s, target, m)))

    out_copies = []

    def hand_over(i):
        if shifts[i]:
            z_copies[i].wait_recv()
        target = lax.rem(c + n - shifts[i], n)
        piece = branch_out.at[pl.ds(pl.multiple_of(m * cut, cut), cut)]
        out_copies.append(send(zin.at[i], piece, out_send.at[i], out_recv.at[m], (other, c, target)))

    project(0)
    share(2)
    project(1)
    share(3)
    combine(0)
    project(2)
    combine(1)
    reduce(0)
    project(3)
    ctx_back = pltpu.make_async_copy(ctx.at[c], ctx_out, local_sem.at[5])
    ctx_back.start()
    combine(2)
    reduce(1)
    hand_over(0)
    reduce(2)
    hand_over(1)
    reduce(3)
    hand_over(3)
    hand_over(2)

    ctx_back.wait()
    for group in qkv_copies + ctx_copies + [z_copies, out_copies]:
        for copy in group:
            copy.wait_send()
    hid_copy.wait()
    for i in range(n):
        for d in range(1, n):
            red_copy(i, d).wait_send()
    for g in range(n):
        pltpu.make_async_remote_copy(
            src_ref=zin.at[0],
            dst_ref=branch_out.at[pl.ds(g * cut, cut)],
            send_sem=out_send.at[0],
            recv_sem=out_recv.at[g],
            device_id=(other, c, g),
            device_id_type=MESH,
        ).wait_recv()


def relay_body(n, hidden, query, keys, values, w_out):
    rows, inner = query.shape[1:]
    depth = hidden.shape[2]
    wide = inner // n
    heads = wide // HEAD_DIM
    cut = -(-depth // (16 * n)) * 16
    bf16 = jnp.bfloat16
    dma = pltpu.SemaphoreType.DMA
    hbm = pl.BlockSpec(memory_space=pltpu.HBM)
    branch, carried, context = pl.pallas_call(
        functools.partial(relay_kernel, n, (2, 1, 3, 0)),
        out_shape=(
            jax.ShapeDtypeStruct((n * cut, rows), bf16),
            jax.ShapeDtypeStruct((depth, rows), bf16),
            jax.ShapeDtypeStruct((rows, inner), bf16),
        ),
        in_specs=[hbm] * 5,
        out_specs=(hbm,) * 3,
        scratch_shapes=[
            pltpu.VMEM((3, rows, inner), bf16),
            pltpu.VMEM((depth, rows), bf16),
            pltpu.VMEM((3, n, rows, wide), bf16),
            pltpu.VMEM((n * cut, inner), bf16),
            pltpu.VMEM((n, heads * rows, n * rows), bf16),
            pltpu.VMEM((n, rows, wide), jnp.float32),
            pltpu.VMEM((n, rows, inner), bf16),
            pltpu.VMEM((n, n, cut, rows), bf16),
            pltpu.VMEM((n, n - 1, cut, rows), bf16),
            pltpu.VMEM((n, cut, rows), bf16),
            pltpu.VMEM((n, cut, rows), bf16),
            dma((6,)),
            dma((3, n - 1)),
            dma((3, n - 1)),
            dma((2,)),
            dma((n, n - 1)),
            dma((n, n - 1)),
            dma((n, n - 1)),
            dma((n, n - 1)),
            dma((n,)),
            dma((n,)),
            dma((n,)),
            dma((n,)),
        ],
        compiler_params=pltpu.CompilerParams(
            collective_id=0, has_side_effects=True, vmem_limit_bytes=60 * 2**20
        ),
    )(query[0], keys[0], values[0], w_out[0], hidden[0].T)
    handed, context = pl.pallas_call(
        finish_kernel,
        out_shape=(
            jax.ShapeDtypeStruct((depth, rows), bf16),
            jax.ShapeDtypeStruct((rows, inner), bf16),
        ),
        in_specs=[hbm] * 3,
        out_specs=(hbm,) * 2,
        scratch_shapes=[pltpu.VMEM((depth, rows), bf16)] * 3 + [pltpu.VMEM((rows, inner), bf16), dma((5,))],
        compiler_params=pltpu.CompilerParams(vmem_limit_bytes=60 * 2**20),
    )(carried, branch, context)
    return (handed.T[None], context[None])


def finish_kernel(carried, branch, context, handed, context_out, first, second, summed, kept, sem):
    depth = handed.shape[0]
    one = pltpu.make_async_copy(carried, first, sem.at[0])
    two = pltpu.make_async_copy(branch.at[pl.ds(0, depth)], second, sem.at[1])
    three = pltpu.make_async_copy(context, kept, sem.at[2])
    for copy in (one, two, three):
        copy.start()
    three.wait()
    last = pltpu.make_async_copy(kept, context_out, sem.at[3])
    last.start()
    one.wait()
    two.wait()
    summed[...] = (first[...].astype(jnp.float32) + second[...].astype(jnp.float32)).astype(jnp.bfloat16)
    result = pltpu.make_async_copy(summed, handed, sem.at[4])
    result.start()
    last.wait()
    result.wait()


def from_behind(block, axis, distance):
    devices = range(lax.axis_size(axis))
    route = [((i - distance) % len(devices), i) for i in devices]
    return lax.ppermute(block, axis, route)


def head_scores(query_h, keys_h):
    return jnp.einsum("qd,kd->qk", query_h, keys_h, preferred_element_type=jnp.float32)


def body(hidden, query, keys, values, w_out):
    n = lax.axis_size("ctx")
    square = lax.axis_size("mp") == n and lax.axis_size("section") == 2
    if square and n == 4 and query.shape[2] % (128 * n) == 0 and query.shape[1] % 128 == 0:
        return relay_body(n, hidden, query, keys, values, w_out)
    rows = hidden[0]
    query_rows = query[0]
    inner_dev = query_rows.shape[1]
    heads_dev = inner_dev // HEAD_DIM
    keys_local = keys[0]
    values_local = values[0]
    keys_all, values_all = (
        lax.all_gather(keys_local, "ctx", axis=0, tiled=True),
        lax.all_gather(values_local, "ctx", axis=0, tiled=True),
    )
    pieces = []
    for head in range(heads_dev):
        lower = head * HEAD_DIM
        upper = lower + HEAD_DIM
        scores = head_scores(query_rows[:, lower:upper], keys_all[:, lower:upper])
        peak = jnp.max(scores, axis=1, keepdims=True)
        expo = jnp.exp(scores - peak)
        total = jnp.sum(expo, axis=1, keepdims=True)
        summed = jnp.dot(
            expo.astype(jnp.bfloat16),
            values_all[:, lower:upper],
            preferred_element_type=jnp.float32,
        )
        pieces.append(summed / total)
    context = jnp.concatenate(pieces, axis=1).astype(jnp.bfloat16)
    out_local = w_out[0]
    context_all = lax.all_gather(context, "ctx", axis=0, tiled=True)
    projected = jnp.einsum(
        "ri,di->rd", context_all, out_local, preferred_element_type=jnp.float32
    ).astype(jnp.bfloat16)
    branch_terms = lax.all_to_all(projected, "ctx", split_axis=0, concat_axis=1, tiled=True).astype(
        jnp.float32
    )
    branch = lax.psum_scatter(
        branch_terms.astype(jnp.bfloat16), "mp", scatter_dimension=1, tiled=True
    ).astype(jnp.float32)
    result = (rows.astype(jnp.float32) + branch).astype(jnp.bfloat16)
    handed = from_behind(result, "section", 1)
    return (handed[None], context[None])


def solution(mesh):
    in_specs = (
        P("section", "ctx", "mp"),
        P("section", "ctx", "mp"),
        P("section", "ctx", "mp"),
        P("section", "ctx", "mp"),
        P("section", "ctx", "mp"),
    )
    out_specs = (P("section", "ctx", "mp"), P("section", "ctx", "mp"))
    return jax.shard_map(body, mesh=mesh, in_specs=in_specs, out_specs=out_specs, check_vma=False)
```

```python
import functools

import jax
import jax.numpy as jnp
from jax import lax
from jax.experimental import pallas as pl
from jax.experimental.pallas import tpu as pltpu
from jax.sharding import PartitionSpec as P

HEAD_DIM = 64
MESH = pl.DeviceIdType.MESH
NT = (((1,), (1,)), ((), ()))


def dot(a, b, dims=(((1,), (0,)), ((), ()))):
    return lax.dot_general(a, b, dims, preferred_element_type=jnp.float32)


def relay_kernel(
    n,
    shifts,
    q_hbm,
    k_hbm,
    v_hbm,
    w_hbm,
    hid_hbm,
    branch_out,
    hid_out,
    ctx_out,
    staged,
    hid,
    qkv,
    w,
    expo,
    total,
    ctx,
    part,
    red,
    zsrc,
    zin,
    local_sem,
    qkv_send,
    qkv_recv,
    hid_sem,
    ctx_send,
    ctx_recv,
    red_send,
    red_recv,
    z_send,
    z_recv,
    out_send,
    out_recv,
):
    s = lax.axis_index("section")
    c = lax.axis_index("ctx")
    m = lax.axis_index("mp")
    other = 1 - s
    x_mate = m + 1 - 2 * lax.rem(m, 2)
    y_mate = lax.rem(m + 2, n)
    first_mate = jnp.where(s == 0, x_mate, y_mate)
    second_mate = jnp.where(s == 0, y_mate, x_mate)

    def mate(d):
        return jnp.where(d == 1, first_mate, jnp.where(d == 2, second_mate, jnp.where(d == 3, n - 1 - m, m)))

    wide = ctx.shape[2] // n
    rows = ctx.shape[1]
    depth = w_hbm.shape[0]
    cut = zsrc.shape[1]

    def columns(j):
        return pl.ds(pl.multiple_of(j * wide, wide), wide)

    def send(src, dst, send_sem, recv_sem, device):
        copy = pltpu.make_async_remote_copy(
            src_ref=src,
            dst_ref=dst,
            send_sem=send_sem,
            recv_sem=recv_sem,
            device_id=device,
            device_id_type=MESH,
        )
        copy.start()
        return copy

    inputs = (k_hbm, q_hbm, v_hbm)
    own = [pltpu.make_async_copy(ref, staged.at[i], local_sem.at[i]) for i, ref in enumerate(inputs)]
    own.append(pltpu.make_async_copy(w_hbm, w.at[pl.ds(0, depth)], local_sem.at[3]))
    own.append(pltpu.make_async_copy(hid_hbm, hid, local_sem.at[4]))
    for copy in own:
        copy.start()

    if n * cut > depth:
        w[depth:] = jnp.zeros((n * cut - depth, w.shape[1]), w.dtype)

    barrier = pltpu.get_barrier_semaphore()
    for d in range(1, n):
        pl.semaphore_signal(barrier, inc=1, device_id=(s, lax.rem(c + d, n), m), device_id_type=MESH)
        pl.semaphore_signal(barrier, inc=1, device_id=(s, c, lax.rem(m + d, n)), device_id_type=MESH)
    for a in range(n):
        pl.semaphore_signal(barrier, inc=1, device_id=(other, c, a), device_id_type=MESH)
    pl.semaphore_wait(barrier, 3 * n - 2)

    qkv_copies = []
    for i in range(3):
        own[i].wait()
        group = []
        for d in range(1, n):
            j = lax.rem(c + d, n)
            group.append(
                send(staged.at[i, :, columns(j)], qkv.at[i, c], qkv_send.at[i, d - 1], qkv_recv.at[i, d - 1], (s, j, m))
            )
        qkv_copies.append(group)
    own[4].wait()
    hid_copy = send(hid, hid_out, hid_sem.at[0], hid_sem.at[1], (other, c, m))
    for i in range(3):
        qkv[i, c] = staged[i, :, columns(c)]

    lane = lax.broadcasted_iota(jnp.int32, (rows, wide), 1) // HEAD_DIM
    heads = wide // HEAD_DIM
    masks = [jnp.where(lane == h, 1.0, 0.0).astype(jnp.bfloat16) for h in range(heads)]
    for i in (0, 1):
        for copy in qkv_copies[i]:
            copy.wait_recv()

    @pl.loop(0, n)
    def _(r):
        keys_all = qkv[0].reshape(n * rows, wide)
        q_r = qkv[1, r]
        scores = dot(jnp.concatenate([q_r * mask for mask in masks], axis=0), keys_all, NT)
        e = jnp.exp(scores - jnp.max(scores, axis=1, keepdims=True))
        sums = jnp.sum(e, axis=1, keepdims=True)
        wide_sum = jnp.broadcast_to(sums[:rows], (rows, wide))
        for h in range(1, heads):
            wide_sum = jnp.where(lane == h, sums[h * rows : (h + 1) * rows], wide_sum)
        total[r] = wide_sum
        expo[r] = e.astype(jnp.bfloat16)

    for copy in qkv_copies[2]:
        copy.wait_recv()

    @pl.loop(0, n)
    def _(r):
        values_all = qkv[2].reshape(n * rows, wide)
        both = dot(expo[r], values_all)
        picked = both[:rows]
        for h in range(1, heads):
            picked = jnp.where(lane == h, both[h * rows : (h + 1) * rows], picked)
        ctx[r, :, columns(c)] = (picked / total[r]).astype(jnp.bfloat16)

    def share(i):
        group = []
        for d in range(1, n):
            j = lax.rem(c + d, n)
            block = ctx.at[lax.rem(j + shifts[i], n), :, columns(c)]
            group.append(send(block, block, ctx_send.at[i, d - 1], ctx_recv.at[i, d - 1], (s, j, m)))
        ctx_copies.append(group)

    ctx_copies = []
    share(0)
    share(1)
    share(2)
    own[3].wait()

    def red_copy(i, d):
        t = mate(d)
        return pltpu.make_async_remote_copy(
            src_ref=part.at[i, t],
            dst_ref=red.at[i, d - 1],
            send_sem=red_send.at[i, d - 1],
            recv_sem=red_recv.at[i, d - 1],
            device_id=(s, c, t),
            device_id_type=MESH,
        )

    def project(i):
        for d in range(1, n):
            block = ctx.at[lax.rem(c + shifts[i], n), :, columns(lax.rem(c + d, n))]
            pltpu.make_async_remote_copy(
                src_ref=block,
                dst_ref=block,
                send_sem=ctx_send.at[i, d - 1],
                recv_sem=ctx_recv.at[i, n - 1 - d],
                device_id=(s, lax.rem(c + d, n), m),
                device_id_type=MESH,
            ).wait_recv()
        r = lax.rem(c + shifts[i], n)

        @pl.loop(1, n + 1)
        def _(d):
            t = mate(d)
            piece = w[pl.ds(pl.multiple_of(t * cut, cut), cut), :]
            part[i, t] = dot(piece, ctx[r], NT).astype(jnp.bfloat16)

            @pl.when(d < n)
            def _():
                red_copy(i, d).start()

    z_copies = []

    def reduce(i):
        for d in range(1, n):
            red_copy(i, d).wait_recv()
        acc = part[i, m].astype(jnp.float32)
        for d in range(1, n):
            acc = acc + red[i, d - 1].astype(jnp.float32)
        if shifts[i] == 0:
            zin[i] = acc.astype(jnp.bfloat16)
        else:
            zsrc[i] = acc.astype(jnp.bfloat16)
            target = lax.rem(c + shifts[i], n)
            z_copies.append(send(zsrc.at[i], zin.at[i], z_send.at[i], z_recv.at[i], (s, target, m)))

    out_copies = []

    def hand_over(i):
        if shifts[i]:
            z_copies[i].wait_recv()
        target = lax.rem(c + n - shifts[i], n)
        piece = branch_out.at[pl.ds(pl.multiple_of(m * cut, cut), cut)]
        out_copies.append(send(zin.at[i], piece, out_send.at[i], out_recv.at[m], (other, c, target)))

    project(0)
    share(3)
    project(1)
    project(2)
    reduce(0)
    project(3)
    reduce(1)
    reduce(2)
    ctx_back = pltpu.make_async_copy(ctx.at[c], ctx_out, local_sem.at[5])
    ctx_back.start()
    hand_over(0)
    hand_over(1)
    reduce(3)
    hand_over(3)
    hand_over(2)

    ctx_back.wait()
    for group in qkv_copies + ctx_copies + [z_copies, out_copies]:
        for copy in group:
            copy.wait_send()
    hid_copy.wait()
    for i in range(n):
        for d in range(1, n):
            red_copy(i, d).wait_send()
    for g in range(n):
        pltpu.make_async_remote_copy(
            src_ref=zin.at[0],
            dst_ref=branch_out.at[pl.ds(g * cut, cut)],
            send_sem=out_send.at[0],
            recv_sem=out_recv.at[g],
            device_id=(other, c, g),
            device_id_type=MESH,
        ).wait_recv()


def relay_body(n, hidden, query, keys, values, w_out):
    rows, inner = query.shape[1:]
    depth = hidden.shape[2]
    wide = inner // n
    heads = wide // HEAD_DIM
    cut = -(-depth // (16 * n)) * 16
    bf16 = jnp.bfloat16
    dma = pltpu.SemaphoreType.DMA
    hbm = pl.BlockSpec(memory_space=pltpu.HBM)
    branch, carried, context = pl.pallas_call(
        functools.partial(relay_kernel, n, (2, 1, 3, 0)),
        out_shape=(
            jax.ShapeDtypeStruct((n * cut, rows), bf16),
            jax.ShapeDtypeStruct((depth, rows), bf16),
            jax.ShapeDtypeStruct((rows, inner), bf16),
        ),
        in_specs=[hbm] * 5,
        out_specs=(hbm,) * 3,
        scratch_shapes=[
            pltpu.VMEM((3, rows, inner), bf16),
            pltpu.VMEM((depth, rows), bf16),
            pltpu.VMEM((3, n, rows, wide), bf16),
            pltpu.VMEM((n * cut, inner), bf16),
            pltpu.VMEM((n, heads * rows, n * rows), bf16),
            pltpu.VMEM((n, rows, wide), jnp.float32),
            pltpu.VMEM((n, rows, inner), bf16),
            pltpu.VMEM((n, n, cut, rows), bf16),
            pltpu.VMEM((n, n - 1, cut, rows), bf16),
            pltpu.VMEM((n, cut, rows), bf16),
            pltpu.VMEM((n, cut, rows), bf16),
            dma((6,)),
            dma((3, n - 1)),
            dma((3, n - 1)),
            dma((2,)),
            dma((n, n - 1)),
            dma((n, n - 1)),
            dma((n, n - 1)),
            dma((n, n - 1)),
            dma((n,)),
            dma((n,)),
            dma((n,)),
            dma((n,)),
        ],
        compiler_params=pltpu.CompilerParams(
            collective_id=0, has_side_effects=True, vmem_limit_bytes=60 * 2**20
        ),
    )(query[0], keys[0], values[0], w_out[0], hidden[0].T)
    handed, context = pl.pallas_call(
        finish_kernel,
        out_shape=(
            jax.ShapeDtypeStruct((depth, rows), bf16),
            jax.ShapeDtypeStruct((rows, inner), bf16),
        ),
        in_specs=[hbm] * 3,
        out_specs=(hbm,) * 2,
        scratch_shapes=[pltpu.VMEM((depth, rows), bf16)] * 3 + [pltpu.VMEM((rows, inner), bf16), dma((5,))],
        compiler_params=pltpu.CompilerParams(vmem_limit_bytes=60 * 2**20),
    )(carried, branch, context)
    return (handed.T[None], context[None])


def finish_kernel(carried, branch, context, handed, context_out, first, second, summed, kept, sem):
    depth = handed.shape[0]
    one = pltpu.make_async_copy(carried, first, sem.at[0])
    two = pltpu.make_async_copy(branch.at[pl.ds(0, depth)], second, sem.at[1])
    three = pltpu.make_async_copy(context, kept, sem.at[2])
    for copy in (one, two, three):
        copy.start()
    three.wait()
    last = pltpu.make_async_copy(kept, context_out, sem.at[3])
    last.start()
    one.wait()
    two.wait()
    summed[...] = (first[...].astype(jnp.float32) + second[...].astype(jnp.float32)).astype(jnp.bfloat16)
    result = pltpu.make_async_copy(summed, handed, sem.at[4])
    result.start()
    last.wait()
    result.wait()


def from_behind(block, axis, distance):
    devices = range(lax.axis_size(axis))
    route = [((i - distance) % len(devices), i) for i in devices]
    return lax.ppermute(block, axis, route)


def head_scores(query_h, keys_h):
    return jnp.einsum("qd,kd->qk", query_h, keys_h, preferred_element_type=jnp.float32)


def body(hidden, query, keys, values, w_out):
    n = lax.axis_size("ctx")
    square = lax.axis_size("mp") == n and lax.axis_size("section") == 2
    if square and n == 4 and query.shape[2] % (128 * n) == 0 and query.shape[1] % 128 == 0:
        return relay_body(n, hidden, query, keys, values, w_out)
    rows = hidden[0]
    query_rows = query[0]
    inner_dev = query_rows.shape[1]
    heads_dev = inner_dev // HEAD_DIM
    keys_local = keys[0]
    values_local = values[0]
    keys_all, values_all = (
        lax.all_gather(keys_local, "ctx", axis=0, tiled=True),
        lax.all_gather(values_local, "ctx", axis=0, tiled=True),
    )
    pieces = []
    for head in range(heads_dev):
        lower = head * HEAD_DIM
        upper = lower + HEAD_DIM
        scores = head_scores(query_rows[:, lower:upper], keys_all[:, lower:upper])
        peak = jnp.max(scores, axis=1, keepdims=True)
        expo = jnp.exp(scores - peak)
        total = jnp.sum(expo, axis=1, keepdims=True)
        summed = jnp.dot(
            expo.astype(jnp.bfloat16),
            values_all[:, lower:upper],
            preferred_element_type=jnp.float32,
        )
        pieces.append(summed / total)
    context = jnp.concatenate(pieces, axis=1).astype(jnp.bfloat16)
    out_local = w_out[0]
    context_all = lax.all_gather(context, "ctx", axis=0, tiled=True)
    projected = jnp.einsum(
        "ri,di->rd", context_all, out_local, preferred_element_type=jnp.float32
    ).astype(jnp.bfloat16)
    branch_terms = lax.all_to_all(projected, "ctx", split_axis=0, concat_axis=1, tiled=True).astype(
        jnp.float32
    )
    branch = lax.psum_scatter(
        branch_terms.astype(jnp.bfloat16), "mp", scatter_dimension=1, tiled=True
    ).astype(jnp.float32)
    result = (rows.astype(jnp.float32) + branch).astype(jnp.bfloat16)
    handed = from_behind(result, "section", 1)
    return (handed[None], context[None])


def solution(mesh):
    in_specs = (
        P("section", "ctx", "mp"),
        P("section", "ctx", "mp"),
        P("section", "ctx", "mp"),
        P("section", "ctx", "mp"),
        P("section", "ctx", "mp"),
    )
    out_specs = (P("section", "ctx", "mp"), P("section", "ctx", "mp"))
    return jax.shard_map(body, mesh=mesh, in_specs=in_specs, out_specs=out_specs, check_vma=False)
```

```python
import functools

import jax
import jax.numpy as jnp
from jax import lax
from jax.experimental import pallas as pl
from jax.experimental.pallas import tpu as pltpu
from jax.sharding import PartitionSpec as P

HEAD_DIM = 64
MESH = pl.DeviceIdType.MESH
NT = (((1,), (1,)), ((), ()))


def dot(a, b, dims=(((1,), (0,)), ((), ()))):
    return lax.dot_general(a, b, dims, preferred_element_type=jnp.float32)


def relay_kernel(
    n,
    shifts,
    q_hbm,
    k_hbm,
    v_hbm,
    w_hbm,
    hid_hbm,
    branch_out,
    hid_out,
    ctx_out,
    staged,
    hid,
    qkv,
    w,
    expo,
    total,
    ctx,
    part,
    red,
    zsrc,
    zin,
    local_sem,
    qkv_send,
    qkv_recv,
    hid_sem,
    ctx_send,
    ctx_recv,
    red_send,
    red_recv,
    z_send,
    z_recv,
    out_send,
    out_recv,
):
    s = lax.axis_index("section")
    c = lax.axis_index("ctx")
    m = lax.axis_index("mp")
    other = 1 - s
    x_mate = m + 1 - 2 * lax.rem(m, 2)
    y_mate = lax.rem(m + 2, n)
    first_mate = jnp.where(s == 0, x_mate, y_mate)
    second_mate = jnp.where(s == 0, y_mate, x_mate)

    def mate(d):
        return jnp.where(d == 1, n - 1 - m, jnp.where(d == 2, first_mate, jnp.where(d == 3, second_mate, m)))

    wide = ctx.shape[2] // n
    rows = ctx.shape[1]
    depth = w_hbm.shape[0]
    cut = zsrc.shape[1]

    def columns(j):
        return pl.ds(pl.multiple_of(j * wide, wide), wide)

    def send(src, dst, send_sem, recv_sem, device):
        copy = pltpu.make_async_remote_copy(
            src_ref=src,
            dst_ref=dst,
            send_sem=send_sem,
            recv_sem=recv_sem,
            device_id=device,
            device_id_type=MESH,
        )
        copy.start()
        return copy

    inputs = (k_hbm, q_hbm, v_hbm)
    own = [pltpu.make_async_copy(ref, staged.at[i], local_sem.at[i]) for i, ref in enumerate(inputs)]
    own.append(pltpu.make_async_copy(w_hbm, w.at[pl.ds(0, depth)], local_sem.at[3]))
    own.append(pltpu.make_async_copy(hid_hbm, hid, local_sem.at[4]))
    for copy in own:
        copy.start()

    if n * cut > depth:
        w[depth:] = jnp.zeros((n * cut - depth, w.shape[1]), w.dtype)

    barrier = pltpu.get_barrier_semaphore()
    for d in range(1, n):
        pl.semaphore_signal(barrier, inc=1, device_id=(s, lax.rem(c + d, n), m), device_id_type=MESH)
        pl.semaphore_signal(barrier, inc=1, device_id=(s, c, lax.rem(m + d, n)), device_id_type=MESH)
    for a in range(n):
        pl.semaphore_signal(barrier, inc=1, device_id=(other, c, a), device_id_type=MESH)
    pl.semaphore_wait(barrier, 3 * n - 2)

    qkv_copies = []
    for i in range(3):
        own[i].wait()
        group = []
        for d in range(1, n):
            j = lax.rem(c + d, n)
            group.append(
                send(staged.at[i, :, columns(j)], qkv.at[i, c], qkv_send.at[i, d - 1], qkv_recv.at[i, d - 1], (s, j, m))
            )
        qkv_copies.append(group)
    own[4].wait()
    hid_copy = send(hid, hid_out, hid_sem.at[0], hid_sem.at[1], (other, c, m))
    for i in range(3):
        qkv[i, c] = staged[i, :, columns(c)]

    lane = lax.broadcasted_iota(jnp.int32, (rows, wide), 1) // HEAD_DIM
    heads = wide // HEAD_DIM
    masks = [jnp.where(lane == h, 1.0, 0.0).astype(jnp.bfloat16) for h in range(heads)]
    for i in (0, 1):
        for copy in qkv_copies[i]:
            copy.wait_recv()

    @pl.loop(0, n)
    def _(r):
        keys_all = qkv[0].reshape(n * rows, wide)
        q_r = qkv[1, r]
        scores = dot(jnp.concatenate([q_r * mask for mask in masks], axis=0), keys_all, NT)
        e = jnp.exp(scores - jnp.max(scores, axis=1, keepdims=True))
        sums = jnp.sum(e, axis=1, keepdims=True)
        wide_sum = jnp.broadcast_to(sums[:rows], (rows, wide))
        for h in range(1, heads):
            wide_sum = jnp.where(lane == h, sums[h * rows : (h + 1) * rows], wide_sum)
        total[r] = wide_sum
        expo[r] = e.astype(jnp.bfloat16)

    for copy in qkv_copies[2]:
        copy.wait_recv()

    @pl.loop(0, n)
    def _(r):
        values_all = qkv[2].reshape(n * rows, wide)
        both = dot(expo[r], values_all)
        picked = both[:rows]
        for h in range(1, heads):
            picked = jnp.where(lane == h, both[h * rows : (h + 1) * rows], picked)
        ctx[r, :, columns(c)] = (picked / total[r]).astype(jnp.bfloat16)

    def share(i):
        group = []
        for d in range(1, n):
            j = lax.rem(c + d, n)
            block = ctx.at[lax.rem(j + shifts[i], n), :, columns(c)]
            group.append(send(block, block, ctx_send.at[i, d - 1], ctx_recv.at[i, d - 1], (s, j, m)))
        ctx_copies.append(group)

    ctx_copies = []
    share(0)
    share(1)
    own[3].wait()

    def red_copy(i, d):
        t = mate(d)
        return pltpu.make_async_remote_copy(
            src_ref=part.at[i, t],
            dst_ref=red.at[i, d - 1],
            send_sem=red_send.at[i, d - 1],
            recv_sem=red_recv.at[i, d - 1],
            device_id=(s, c, t),
            device_id_type=MESH,
        )

    def project(i):
        for d in range(1, n):
            block = ctx.at[lax.rem(c + shifts[i], n), :, columns(lax.rem(c + d, n))]
            pltpu.make_async_remote_copy(
                src_ref=block,
                dst_ref=block,
                send_sem=ctx_send.at[i, d - 1],
                recv_sem=ctx_recv.at[i, n - 1 - d],
                device_id=(s, lax.rem(c + d, n), m),
                device_id_type=MESH,
            ).wait_recv()
        r = lax.rem(c + shifts[i], n)

        @pl.loop(1, n + 1)
        def _(d):
            t = mate(d)
            piece = w[pl.ds(pl.multiple_of(t * cut, cut), cut), :]
            part[i, t] = dot(piece, ctx[r], NT).astype(jnp.bfloat16)

            @pl.when(d < n)
            def _():
                red_copy(i, d).start()

    z_copies = []

    def reduce(i):
        for d in range(1, n):
            red_copy(i, d).wait_recv()
        acc = part[i, m].astype(jnp.float32)
        for d in range(1, n):
            acc = acc + red[i, d - 1].astype(jnp.float32)
        if shifts[i] == 0:
            zin[i] = acc.astype(jnp.bfloat16)
        else:
            zsrc[i] = acc.astype(jnp.bfloat16)
            target = lax.rem(c + shifts[i], n)
            z_copies.append(send(zsrc.at[i], zin.at[i], z_send.at[i], z_recv.at[i], (s, target, m)))

    out_copies = []

    def hand_over(i):
        if shifts[i]:
            z_copies[i].wait_recv()
        target = lax.rem(c + n - shifts[i], n)
        piece = branch_out.at[pl.ds(pl.multiple_of(m * cut, cut), cut)]
        out_copies.append(send(zin.at[i], piece, out_send.at[i], out_recv.at[m], (other, c, target)))

    project(0)
    for i in range(2, n):
        share(i)
        project(i - 1)
        if i > 2:
            reduce(i - 3)
    project(n - 1)
    ctx_back = pltpu.make_async_copy(ctx.at[c], ctx_out, local_sem.at[5])
    ctx_back.start()
    for i in range(n - 3, n):
        reduce(i)
        if i < n - 1:
            hand_over(i - 1)
    hand_over(n - 1)
    hand_over(n - 2)

    ctx_back.wait()
    for group in qkv_copies + ctx_copies + [z_copies, out_copies]:
        for copy in group:
            copy.wait_send()
    hid_copy.wait()
    for i in range(n):
        for d in range(1, n):
            red_copy(i, d).wait_send()
    for g in range(n):
        pltpu.make_async_remote_copy(
            src_ref=zin.at[0],
            dst_ref=branch_out.at[pl.ds(g * cut, cut)],
            send_sem=out_send.at[0],
            recv_sem=out_recv.at[g],
            device_id=(other, c, g),
            device_id_type=MESH,
        ).wait_recv()


def relay_body(n, hidden, query, keys, values, w_out):
    rows, inner = query.shape[1:]
    depth = hidden.shape[2]
    wide = inner // n
    heads = wide // HEAD_DIM
    cut = -(-depth // (16 * n)) * 16
    bf16 = jnp.bfloat16
    dma = pltpu.SemaphoreType.DMA
    hbm = pl.BlockSpec(memory_space=pltpu.HBM)
    branch, carried, context = pl.pallas_call(
        functools.partial(relay_kernel, n, (2, 1, 3, 0)),
        out_shape=(
            jax.ShapeDtypeStruct((n * cut, rows), bf16),
            jax.ShapeDtypeStruct((depth, rows), bf16),
            jax.ShapeDtypeStruct((rows, inner), bf16),
        ),
        in_specs=[hbm] * 5,
        out_specs=(hbm,) * 3,
        scratch_shapes=[
            pltpu.VMEM((3, rows, inner), bf16),
            pltpu.VMEM((depth, rows), bf16),
            pltpu.VMEM((3, n, rows, wide), bf16),
            pltpu.VMEM((n * cut, inner), bf16),
            pltpu.VMEM((n, heads * rows, n * rows), bf16),
            pltpu.VMEM((n, rows, wide), jnp.float32),
            pltpu.VMEM((n, rows, inner), bf16),
            pltpu.VMEM((n, n, cut, rows), bf16),
            pltpu.VMEM((n, n - 1, cut, rows), bf16),
            pltpu.VMEM((n, cut, rows), bf16),
            pltpu.VMEM((n, cut, rows), bf16),
            dma((6,)),
            dma((3, n - 1)),
            dma((3, n - 1)),
            dma((2,)),
            dma((n, n - 1)),
            dma((n, n - 1)),
            dma((n, n - 1)),
            dma((n, n - 1)),
            dma((n,)),
            dma((n,)),
            dma((n,)),
            dma((n,)),
        ],
        compiler_params=pltpu.CompilerParams(
            collective_id=0, has_side_effects=True, vmem_limit_bytes=60 * 2**20
        ),
    )(query[0], keys[0], values[0], w_out[0], hidden[0].T)
    handed, context = pl.pallas_call(
        finish_kernel,
        out_shape=(
            jax.ShapeDtypeStruct((depth, rows), bf16),
            jax.ShapeDtypeStruct((rows, inner), bf16),
        ),
        in_specs=[hbm] * 3,
        out_specs=(hbm,) * 2,
        scratch_shapes=[pltpu.VMEM((depth, rows), bf16)] * 3 + [pltpu.VMEM((rows, inner), bf16), dma((5,))],
        compiler_params=pltpu.CompilerParams(vmem_limit_bytes=60 * 2**20),
    )(carried, branch, context)
    return (handed.T[None], context[None])


def finish_kernel(carried, branch, context, handed, context_out, first, second, summed, kept, sem):
    depth = handed.shape[0]
    one = pltpu.make_async_copy(carried, first, sem.at[0])
    two = pltpu.make_async_copy(branch.at[pl.ds(0, depth)], second, sem.at[1])
    three = pltpu.make_async_copy(context, kept, sem.at[2])
    for copy in (one, two, three):
        copy.start()
    three.wait()
    last = pltpu.make_async_copy(kept, context_out, sem.at[3])
    last.start()
    one.wait()
    two.wait()
    summed[...] = (first[...].astype(jnp.float32) + second[...].astype(jnp.float32)).astype(jnp.bfloat16)
    result = pltpu.make_async_copy(summed, handed, sem.at[4])
    result.start()
    last.wait()
    result.wait()


def from_behind(block, axis, distance):
    devices = range(lax.axis_size(axis))
    route = [((i - distance) % len(devices), i) for i in devices]
    return lax.ppermute(block, axis, route)


def head_scores(query_h, keys_h):
    return jnp.einsum("qd,kd->qk", query_h, keys_h, preferred_element_type=jnp.float32)


def body(hidden, query, keys, values, w_out):
    n = lax.axis_size("ctx")
    square = lax.axis_size("mp") == n and lax.axis_size("section") == 2
    if square and n == 4 and query.shape[2] % (128 * n) == 0 and query.shape[1] % 128 == 0:
        return relay_body(n, hidden, query, keys, values, w_out)
    rows = hidden[0]
    query_rows = query[0]
    inner_dev = query_rows.shape[1]
    heads_dev = inner_dev // HEAD_DIM
    keys_local = keys[0]
    values_local = values[0]
    keys_all, values_all = (
        lax.all_gather(keys_local, "ctx", axis=0, tiled=True),
        lax.all_gather(values_local, "ctx", axis=0, tiled=True),
    )
    pieces = []
    for head in range(heads_dev):
        lower = head * HEAD_DIM
        upper = lower + HEAD_DIM
        scores = head_scores(query_rows[:, lower:upper], keys_all[:, lower:upper])
        peak = jnp.max(scores, axis=1, keepdims=True)
        expo = jnp.exp(scores - peak)
        total = jnp.sum(expo, axis=1, keepdims=True)
        summed = jnp.dot(
            expo.astype(jnp.bfloat16),
            values_all[:, lower:upper],
            preferred_element_type=jnp.float32,
        )
        pieces.append(summed / total)
    context = jnp.concatenate(pieces, axis=1).astype(jnp.bfloat16)
    out_local = w_out[0]
    context_all = lax.all_gather(context, "ctx", axis=0, tiled=True)
    projected = jnp.einsum(
        "ri,di->rd", context_all, out_local, preferred_element_type=jnp.float32
    ).astype(jnp.bfloat16)
    branch_terms = lax.all_to_all(projected, "ctx", split_axis=0, concat_axis=1, tiled=True).astype(
        jnp.float32
    )
    branch = lax.psum_scatter(
        branch_terms.astype(jnp.bfloat16), "mp", scatter_dimension=1, tiled=True
    ).astype(jnp.float32)
    result = (rows.astype(jnp.float32) + branch).astype(jnp.bfloat16)
    handed = from_behind(result, "section", 1)
    return (handed[None], context[None])


def solution(mesh):
    in_specs = (
        P("section", "ctx", "mp"),
        P("section", "ctx", "mp"),
        P("section", "ctx", "mp"),
        P("section", "ctx", "mp"),
        P("section", "ctx", "mp"),
    )
    out_specs = (P("section", "ctx", "mp"), P("section", "ctx", "mp"))
    return jax.shard_map(body, mesh=mesh, in_specs=in_specs, out_specs=out_specs, check_vma=False)
```
